256 devices in a mesh: dp: 16 (over x_lo, z), ctx: 16 (over x_hi, y, core).
Axes of the slice: x: 4 (x_hi: 2, x_lo: 2; x = x_hi * 2 + x_lo), y: 4, z: 8, core: 2. Of those that a mesh axis runs over, the one named last changes fastest.
Arguments:
- queries: bfloat16 [16, 2304, 1024], P('dp', 'ctx'), may hold values from -6 to 6
- keys: bfloat16 [16, 2304, 1024], P('dp', 'ctx'), may hold values from -6 to 6
- values: bfloat16 [16, 2304, 1024], P('dp', 'ctx'), may hold values from -6 to 6
- gates: bfloat16 [16, 2304, 1024], P('dp', 'ctx'), may hold values from -6 to 6
- attn_out: bfloat16 [16, 2304, 1024], P('dp', 'ctx'), may hold values from -6 to 6
- grad_out: bfloat16 [16, 2304, 1024], P('dp', 'ctx'), may hold values from -6 to 6
- route: int32 [16, 256], P('dp', 'ctx'), may hold values from 0 to 15, as said below
- lengths: int32 [16, 4], P('dp'), may hold values from 1 to 1152, 2304 in all within a row
Outputs:
- grad_queries: bfloat16 [16, 2304, 1024], P('dp', 'ctx')
- grad_keys: bfloat16 [16, 2304, 1024], P('dp', 'ctx')
- grad_values: bfloat16 [16, 2304, 1024], P('dp', 'ctx')
- grad_gates: bfloat16 [16, 2304, 1024], P('dp', 'ctx')
The draws below stay inside these ranges and needn't reach their ends.
Inputs may be any that keep to these rules, and one draw needn't show every extreme that they name: In each row of route, each aligned block of 16 entries starting at a multiple of 16 names every bucket stream once. Each row of lengths sums to 2304, and its largest entry is 1152.
All inputs are finite; a program needn't handle non-finite values.
Results may differ from the reference program's by a relative error of at most 0.0058.
Values may be sent and summed in bfloat16 or wider, within the bound.
A program may use at most 128 MiB of HBM per device.

```python
import math
import jax
import jax.numpy as jnp
import numpy as np
from jax import lax

D = 1024
HEADS = 8
HEAD_DIM = 128
TOK_DEV = 144
USERS = 4
ATT_DIV = 32
L = 2304
BLK = 9
N_DP = 16
N_CTX = 16


def draw_route(key, part):
    key = jax.random.fold_in(key, 7)
    row_keys = jax.random.split(key, N_DP * N_CTX)
    perms = jax.vmap(lambda row_key: jax.random.permutation(row_key, N_DP))(row_keys)
    return perms.reshape(N_DP, N_CTX * N_DP).astype(jnp.int32)


def levels(stream_key, dims, shards, smallest, largest):
    loudness = 1.0
    for position, shards_of in shards:
        steps = jax.random.uniform(jax.random.fold_in(jax.random.fold_in(stream_key, 6), position), (shards_of,), jnp.float32, smallest / len(shards), largest / len(shards))
        loudness = loudness * jnp.repeat(jnp.exp(steps), dims[position] // shards_of).reshape((-1,) + (1,) * (len(dims) - 1 - position))
    return loudness


def profile(amount, total, reach, slope):
    portions = [(1 << 20) // math.isqrt(grade ** slope) + 1 for grade in range(2, amount + 1)]
    surplus, holding = total - reach - (amount - 1), [1] * (amount - 1)
    while surplus > 0:
        movable = [i for i in range(amount - 1) if holding[i] < reach]
        whole, left = sum([portions[i] for i in movable]), surplus
        for i in movable:
            more = min(reach - holding[i], max(1, left * portions[i] // whole), surplus)
            holding[i] = holding[i] + more
            surplus = surplus - more
    return np.array([reach] + holding)


def uneven_parts(own_key, count, total, bound, slope):
    if count == 2:
        one = jax.random.randint(own_key, (), max(1, total - bound), min(bound, total - 1) + 1)
        return jnp.stack([one, total - one])
    tallies = jnp.asarray(profile(count, total, bound, slope), jnp.int32)
    pairs = (count - 1) // 2
    donor, receiver = tallies[1:1 + 2 * pairs:2], tallies[2:2 + 2 * pairs:2]
    room = jnp.minimum(donor - 1, bound - receiver)
    moved = jax.random.randint(jax.random.fold_in(own_key, 1), (pairs,), 0, 1 << 20) % (room + 1)
    tallies = tallies.at[1:1 + 2 * pairs:2].set(donor - moved).at[2:2 + 2 * pairs:2].set(receiver + moved)
    return tallies[jax.random.permutation(jax.random.fold_in(own_key, 2), count)]


def normal_values(stream_key, dims, deviation, reach, cuts=(), kind=jnp.bfloat16):
    values = jax.random.normal(stream_key, dims, jnp.float32) * deviation
    if len(cuts) > 0:
        values = levels(stream_key, dims, cuts, -0.22, 0.18) * values
    return jnp.clip(values, min=-reach, max=reach).astype(kind)


def setup_inputs(seed: int = 0) -> dict:
    key_list = jax.random.split(jax.random.key(seed), 9)
    return {
        "queries": normal_values(key_list[0], (N_DP, L, D), 1.0, 6.0, ((0, 16), (1, 16))),
        "keys": normal_values(key_list[1], (N_DP, L, D), 1.0, 6.0, ((0, 16), (1, 16))),
        "values": normal_values(key_list[2], (N_DP, L, D), 1.0, 6.0, ((0, 16), (1, 16))),
        "gates": normal_values(key_list[3], (N_DP, L, D), 1.0, 6.0, ((0, 16), (1, 16))),
        "attn_out": normal_values(key_list[4], (N_DP, L, D), 1.0, 6.0, ((0, 16), (1, 16))),
        "grad_out": normal_values(key_list[5], (N_DP, L, D), 1.0, 6.0, ((0, 16), (1, 16))),
        "route": draw_route(jax.random.fold_in(key_list[8], 71), 0),
        "lengths": jax.vmap(lambda own: uneven_parts(own, USERS, L, L // 2, 2))(jax.random.split(key_list[7], N_DP)).reshape((N_DP, USERS)).astype(jnp.int32),
    }


def regroup(array, route):
    blocks = array.reshape(N_DP, N_CTX, N_DP, BLK, D)
    targets = route.reshape(N_DP, N_CTX, N_DP)
    sources = jnp.argsort(targets, axis=2).astype(jnp.int32)
    picked = jnp.take_along_axis(blocks, sources[:, :, :, None, None], axis=2)
    return jnp.transpose(picked, (2, 1, 0, 3, 4)).reshape(N_DP, L, D)

def ungroup(array, route):
    blocks = jnp.transpose(array.reshape(N_DP, N_CTX, N_DP, BLK, D), (2, 1, 0, 3, 4))
    targets = route.reshape(N_DP, N_CTX, N_DP).astype(jnp.int32)
    picked = jnp.take_along_axis(blocks, targets[:, :, :, None, None], axis=2)
    return picked.reshape(N_DP, L, D)

def place_of(rows):
    half_rows = TOK_DEV // 2
    shard = rows // TOK_DEV
    inner = rows % TOK_DEV
    early = shard * half_rows + inner
    late = (2 * N_CTX - 1 - shard) * half_rows + inner - half_rows
    return jnp.where(inner < half_rows, early, late).astype(jnp.int32)

def attend(q_heads, k_heads, v_heads, do_heads, live_mask, score_scale):
    q_full = q_heads.astype(jnp.float32)
    k_full = k_heads.astype(jnp.float32)
    v_full = v_heads.astype(jnp.float32)
    do_full = do_heads.astype(jnp.float32)
    scores = jnp.einsum('phd,rhd->hpr', q_full, k_full) * score_scale
    sig_val = jax.nn.sigmoid(scores)
    weight = (live_mask[None] * scores * sig_val / ATT_DIV).astype(jnp.bfloat16)
    dweight = jnp.einsum('phd,rhd->hpr', do_full, v_full)
    dscore = (live_mask[None] * dweight * sig_val * (1.0 + scores * (1.0 - sig_val)) / ATT_DIV).astype(jnp.bfloat16)
    grad_v = jnp.einsum('hpr,phd->rhd', weight.astype(jnp.float32), do_full)
    grad_q = jnp.einsum('hpr,rhd->phd', dscore.astype(jnp.float32), k_full) * score_scale
    grad_k = jnp.einsum('hpr,phd->rhd', dscore.astype(jnp.float32), q_full) * score_scale
    return (grad_q, grad_k, grad_v)

def one_stream(inputs):
    q_rows, k_rows, v_rows, u_rows, o_rows, dy_rows, user_lengths = inputs
    score_scale = 1.0 / math.sqrt(HEAD_DIM)
    o_full = o_rows.astype(jnp.float32)
    row_mean = lax.optimization_barrier(jnp.mean(o_full, axis=1, keepdims=True))
    centred = o_full - row_mean
    inv_std = 1.0 / jnp.sqrt(lax.optimization_barrier(jnp.mean(centred * centred, axis=1, keepdims=True)) + 1e-05)
    normed = centred * inv_std
    dy_full = dy_rows.astype(jnp.float32)
    grad_u = (dy_full * normed).astype(jnp.bfloat16)
    g_term = dy_full * u_rows.astype(jnp.float32)
    d_o = (inv_std * (g_term - lax.optimization_barrier(jnp.mean(g_term, axis=1, keepdims=True)) - normed * lax.optimization_barrier(jnp.mean(g_term * normed, axis=1, keepdims=True)))).astype(jnp.bfloat16)
    user_ends = jnp.cumsum(user_lengths)
    positions = place_of(jnp.arange(L, dtype=jnp.int32))
    segments = lax.optimization_barrier(jnp.sum((positions[:, None] >= user_ends[None, :]).astype(jnp.int32), axis=1))
    q_heads = q_rows.reshape(L, HEADS, HEAD_DIM)
    k_heads = k_rows.reshape(L, HEADS, HEAD_DIM)
    v_heads = v_rows.reshape(L, HEADS, HEAD_DIM)
    do_heads = d_o.reshape(L, HEADS, HEAD_DIM)

    def query_block(state, block_index):
        dk_sum, dv_sum = state
        start = (block_index * TOK_DEV).astype(jnp.int32)
        q_part = lax.dynamic_slice_in_dim(q_heads, start, TOK_DEV, 0)
        do_part = lax.dynamic_slice_in_dim(do_heads, start, TOK_DEV, 0)
        q_pos = lax.dynamic_slice_in_dim(positions, start, TOK_DEV, 0)
        q_seg = lax.dynamic_slice_in_dim(segments, start, TOK_DEV, 0)
        live_mask = ((q_seg[:, None] == segments[None, :]) & (positions[None, :] <= q_pos[:, None])).astype(jnp.float32)
        grad_q, grad_k, grad_v = attend(q_part, k_heads, v_heads, do_part, live_mask, score_scale)
        return ((dk_sum + grad_k, dv_sum + grad_v), grad_q)
    zero_heads = jnp.zeros((L, HEADS, HEAD_DIM), jnp.float32)
    (dk_sum, dv_sum), dq_parts = lax.scan(query_block, (zero_heads, zero_heads), jnp.arange(N_CTX, dtype=jnp.int32))
    grad_q = dq_parts.reshape(L, D).astype(jnp.bfloat16)
    return (grad_q, dk_sum.reshape(L, D).astype(jnp.bfloat16), dv_sum.reshape(L, D).astype(jnp.bfloat16), grad_u)

def reference(queries, keys, values, gates, attn_out, grad_out, route, lengths):
    bucketed = tuple((regroup(array, route) for array in (queries, keys, values, gates, attn_out, grad_out)))
    grad_q, grad_k, grad_v, grad_u = lax.map(one_stream, bucketed + (lengths,))
    return (ungroup(grad_q, route), ungroup(grad_k, route), ungroup(grad_v, route), ungroup(grad_u, route))
```

```python
import math

import jax
import jax.numpy as jnp
from jax import lax
from jax.experimental import pallas as pl
from jax.experimental.pallas import tpu as pltpu
from jax.sharding import PartitionSpec as P

D = 1024
HEADS = 8
HD = 128
ROWS = 144
HALF = 72
PADH = 80
BLK = 9
NDP = 16
NZ = 8
NCTX = 16
NM = 8
USERS = 4
ATT_DIV = 32
RT = 160
PB = 256
NRT = 8
NPB = 10
MESH = pl.DeviceIdType.MESH
F32 = jnp.float32
BF16 = jnp.bfloat16
NT = (((1,), (1,)), ((), ()))


def p_blocks(rt):
    return (rt, NPB) if rt < 4 else (5, 7 + rt - 4)


def kernel(
    tgt, lens, q_ref, k_ref, v_ref, u_ref, o_ref, dy_ref,
    oq_ref, ok_ref, ov_ref, ou_ref,
    scr, sb_qk, rb_qk, sb_1, rb_1, sa, qd, kv, w_buf, f_buf, ds_buf,
    dq_buf, xs, xr, g2, r2, sb2, rb2,
    ss_b, rs_b, ss_a, rs_a, ss_f, rs_f, ss_x, rs_x, ss_a2, rs_a2, ss_b2, rs_b2,
):
    dp = lax.axis_index("dp")
    ctx = lax.axis_index("ctx")
    xlo, z = dp // NZ, dp % NZ
    m, kap = ctx // 2, ctx % 2
    scale = 1.0 / math.sqrt(HD)

    def dp_peer(d):
        return ((xlo + d) % 2) * NZ + (z + d // 2) % NZ

    def m_peer(e):
        return (m + e) % NM

    barrier = pltpu.get_barrier_semaphore()

    def greet_dp(d, c):
        pl.semaphore_signal(barrier, inc=1, device_id=(dp_peer(d), ctx), device_id_type=MESH)
        return c

    def greet_m(e, c):
        pl.semaphore_signal(barrier, inc=1, device_id=(dp, m_peer(e) * 2 + kap), device_id_type=MESH)
        return c

    lax.fori_loop(1, NDP, greet_dp, 0)
    lax.fori_loop(1, NM, greet_m, 0)
    pl.semaphore_signal(barrier, inc=1, device_id=(dp, m * 2 + 1 - kap), device_id_type=MESH)

    row = lax.broadcasted_iota(jnp.int32, (ROWS, ROWS), 0)
    col = lax.broadcasted_iota(jnp.int32, (ROWS, ROWS), 1)
    shift_c = jnp.zeros((ROWS, ROWS), jnp.int32)
    shift_r = jnp.zeros((ROWS, ROWS), jnp.int32)
    for b in range(NDP):
        by = (tgt[0, b] - b) * BLK
        shift_c = jnp.where((col >= b * BLK) & (col < b * BLK + BLK), by, shift_c)
        shift_r = jnp.where((row >= b * BLK) & (row < b * BLK + BLK), by, shift_r)
    to_stream = jnp.where(row == col + shift_c, 1.0, 0.0).astype(BF16)
    to_arrival = jnp.where(col == row + shift_r, 1.0, 0.0).astype(BF16)

    def pack_b(arrays, dst):
        n = len(arrays) * HEADS
        for a, x in enumerate(arrays):
            y = jnp.dot(to_stream, x, preferred_element_type=F32)
            for h in range(HEADS):
                scr[pl.ds(a * HEADS + h, ROWS, stride=n), :] = y[:, h * HD:(h + 1) * HD]
        size = dst.shape[1]
        for j in range(NDP):
            dst[j] = scr[j * BLK * n:j * BLK * n + size, :].astype(BF16)

    def copy_b(src, dst, ch, peer, ssem, rsem):
        return pltpu.make_async_remote_copy(
            src_ref=src.at[peer], dst_ref=dst.at[dp], send_sem=ssem.at[ch, peer], recv_sem=rsem.at[ch, dp],
            device_id=(peer, ctx), device_id_type=MESH)

    def arrival_b(src, dst, ch, peer, ssem, rsem):
        return pltpu.make_async_remote_copy(
            src_ref=src.at[peer], dst_ref=dst.at[peer], send_sem=ssem.at[ch, peer], recv_sem=rsem.at[ch, peer],
            device_id=(peer, ctx), device_id_type=MESH)

    def send_b(src, dst, ch, ssem, rsem):
        def step(d, c):
            copy_b(src, dst, ch, dp_peer(d), ssem, rsem).start()
            return c

        lax.fori_loop(1, NDP, step, 0)
        dst[dp] = src[dp]

    def wait_b(src, dst, ch, ssem, rsem):
        def step(d, c):
            arrival_b(src, dst, ch, dp_peer(d), ssem, rsem).wait_recv()
            return c

        lax.fori_loop(1, NDP, step, 0)

    def drain_b(src, dst, ch, ssem, rsem):
        def step(d, c):
            copy_b(src, dst, ch, dp_peer(d), ssem, rsem).wait_send()
            return c

        lax.fori_loop(1, NDP, step, 0)

    zeros8 = jnp.zeros((PADH - HALF, HD), F32)

    def pack_a(src, arrays):
        n = len(arrays) * HEADS
        for i in range(NDP):
            scr[i * BLK * n:(i + 1) * BLK * n, :] = src[i][:BLK * n].astype(F32)
        for a, arr in enumerate(arrays):
            for h in range(HEADS):
                x = scr[pl.ds(a * HEADS + h, ROWS, stride=n), :]
                sa[arr, h, 0] = jnp.concatenate([x[:HALF], zeros8], axis=0).astype(BF16)
                sa[arr, h, 1] = jnp.concatenate([x[HALF:], zeros8], axis=0).astype(BF16)

    def slot_a(arr, mm):
        return qd.at[arr // 2, :, mm * 2 + kap] if arr % 2 == 0 else kv.at[arr // 2, :, mm]

    def copy_a(arr, peer):
        return pltpu.make_async_remote_copy(
            src_ref=sa.at[arr, peer], dst_ref=slot_a(arr, m), send_sem=ss_a.at[arr, peer], recv_sem=rs_a.at[arr, m],
            device_id=(dp, peer * 2 + kap), device_id_type=MESH)

    def arrival_a(arr, peer):
        return pltpu.make_async_remote_copy(
            src_ref=sa.at[arr, peer], dst_ref=slot_a(arr, peer), send_sem=ss_a.at[arr, peer], recv_sem=rs_a.at[arr, peer],
            device_id=(dp, peer * 2 + kap), device_id_type=MESH)

    def send_a(arr):
        def step(e, c):
            copy_a(arr, m_peer(e)).start()
            return c

        lax.fori_loop(1, NM, step, 0)
        if arr % 2 == 0:
            qd[arr // 2, :, ctx] = sa[arr, m]
        else:
            kv[arr // 2, :, m] = sa[arr, m]

    def copy_f(a, mm, par):
        ref = qd.at[a, :, mm * 2 + par]
        return pltpu.make_async_remote_copy(
            src_ref=ref, dst_ref=ref, send_sem=ss_f.at[a, mm], recv_sem=rs_f.at[a, mm],
            device_id=(dp, m * 2 + 1 - kap), device_id_type=MESH)

    def wait_a(arr):
        def step(e, c):
            arrival_a(arr, m_peer(e)).wait_recv()
            if arr % 2 == 0:
                copy_f(arr // 2, m_peer(e), kap).start()
            return c

        if arr % 2 == 0:
            copy_f(arr // 2, m, kap).start()
        lax.fori_loop(1, NM, step, 0)

    def wait_f(a):
        def step(e, c):
            copy_f(a, m_peer(e), 1 - kap).wait_recv()
            return c

        lax.fori_loop(0, NM, step, 0)

    pack_b([q_ref[...], k_ref[...]], sb_qk)
    pl.semaphore_wait(barrier, NDP - 1 + NM - 1 + 1)
    send_b(sb_qk, rb_qk, 0, ss_b, rs_b)

    o_full = o_ref[...].astype(F32)
    centred = o_full - jnp.mean(o_full, axis=1, keepdims=True)
    inv_std = 1.0 / jnp.sqrt(jnp.mean(centred * centred, axis=1, keepdims=True) + 1e-05)
    normed = centred * inv_std
    dy_full = dy_ref[...].astype(F32)
    ou_ref[...] = (dy_full * normed).astype(BF16)
    g_term = dy_full * u_ref[...].astype(F32)
    d_o = inv_std * (
        g_term
        - jnp.mean(g_term, axis=1, keepdims=True)
        - normed * jnp.mean(g_term * normed, axis=1, keepdims=True)
    )
    pack_b([d_o.astype(BF16)], sb_1.at[0])
    send_b(sb_1.at[0], rb_1.at[0], 1, ss_b, rs_b)
    pack_b([v_ref[...]], sb_1.at[1])
    send_b(sb_1.at[1], rb_1.at[1], 2, ss_b, rs_b)

    wait_b(sb_qk, rb_qk, 0, ss_b, rs_b)
    pack_a(rb_qk, [0, 1])
    send_a(0)
    send_a(1)

    lane = lax.broadcasted_iota(jnp.int32, (8, PB), 1)
    sub = lax.broadcasted_iota(jnp.int32, (RT, PB), 0)
    ends = []
    total = jnp.int32(0)
    for user in range(USERS):
        total = total + lens[0, user]
        ends.append(total)

    def query_places(b):
        lane_at = lane + b * PB
        late = lane_at >= NCTX * PADH
        lane_in = lane_at - jnp.where(late, NCTX * PADH, 0)
        chunk = jnp.zeros_like(lane_in)
        for c in range(1, NCTX):
            chunk = chunk + jnp.where(lane_in >= c * PADH, 1, 0)
        inner = lane_in - chunk * PADH
        place = jnp.where(late, 2 * NCTX - 1 - chunk, chunk) * HALF + inner
        first = jnp.zeros_like(place)
        for user in range(USERS - 1):
            first = jnp.maximum(first, jnp.where(ends[user] <= place, ends[user], 0))
        return place[:1], first[:1]

    def key_places(rt):
        t = rt % 4
        second = sub >= PADH
        c = 2 * (2 * t + jnp.where(second, 1, 0)) + kap
        chunk = c if rt < 4 else 2 * NCTX - 1 - c
        return chunk * HALF + sub - jnp.where(second, PADH, 0)

    def q_at(a, b):
        return qd.at[a].reshape(2 * NCTX * PADH, HD)[pl.ds(pl.multiple_of(b * PB, PB), PB), :]

    def k_at(a, rt):
        return kv.at[a].reshape(2 * NM * PADH, HD)[rt * RT:(rt + 1) * RT, :]

    wait_a(0)
    wait_a(1)
    wait_f(0)

    for rt in range(NRT):
        keys = k_at(0, rt)
        key_place = key_places(rt)

        def score_step(b, c, rt=rt, keys=keys, key_place=key_place):
            place, first = query_places(b)
            s = lax.dot_general(keys, q_at(0, b), NT, preferred_element_type=F32) * scale
            sig = 0.5 * jnp.tanh(0.5 * s) + 0.5
            sig = jnp.where((key_place <= place) & (key_place >= first), sig, 0.0)
            w = s * sig
            w_buf[rt, b] = w.astype(BF16)
            f_buf[rt, b] = sig * (1.0 - w) + w
            return c

        lax.fori_loop(*p_blocks(rt), score_step, 0)

    wait_b(sb_1.at[0], rb_1.at[0], 1, ss_b, rs_b)
    pack_a(rb_1.at[0], [2])
    send_a(2)
    wait_a(2)
    wait_f(1)

    def copy_a2(g, peer):
        return pltpu.make_async_remote_copy(
            src_ref=g2.at[g, peer], dst_ref=r2.at[g, m], send_sem=ss_a2.at[g, peer], recv_sem=rs_a2.at[g, m],
            device_id=(dp, peer * 2 + kap), device_id_type=MESH)

    def arrival_a2(g, peer):
        return pltpu.make_async_remote_copy(
            src_ref=g2.at[g, peer], dst_ref=r2.at[g, peer], send_sem=ss_a2.at[g, peer], recv_sem=rs_a2.at[g, peer],
            device_id=(dp, peer * 2 + kap), device_id_type=MESH)

    def send_a2(g):
        def step(e, c):
            copy_a2(g, m_peer(e)).start()
            return c

        lax.fori_loop(1, NM, step, 0)
        r2[g, m] = g2[g, m]

    def send_b2(g):
        def step(e, c):
            arrival_a2(g, m_peer(e)).wait_recv()
            return c

        lax.fori_loop(1, NM, step, 0)
        for h in range(HEADS):
            scr[pl.ds(h, HALF, stride=HEADS), :] = r2[g, h, 0].astype(F32)[:HALF]
            scr[pl.ds(HALF * HEADS + h, HALF, stride=HEADS), :] = r2[g, h, 1].astype(F32)[:HALF]
        for i in range(NDP):
            sb2[g, i] = scr[i * HALF:i * HALF + PADH, :].astype(BF16)
        send_b(sb2.at[g], rb2.at[g], g, ss_b2, rs_b2)

    def put_keys_grad(g, rt, value):
        t, half = rt % 4, rt // 4
        g2[g, 2 * t, half] = value[:PADH].astype(BF16)
        g2[g, 2 * t + 1, half] = value[PADH:].astype(BF16)

    for rt in range(NRT):
        def dv_step(b, acc, rt=rt):
            return acc + jnp.dot(w_buf[rt, b], q_at(1, b), preferred_element_type=F32)

        acc = lax.fori_loop(*p_blocks(rt), dv_step, jnp.zeros((RT, HD), F32))
        put_keys_grad(0, rt, acc * (1.0 / ATT_DIV))
    send_a2(0)

    wait_b(sb_1.at[1], rb_1.at[1], 2, ss_b, rs_b)
    pack_a(rb_1.at[1], [3])
    send_a(3)
    send_b2(0)
    wait_a(3)

    for rt in range(NRT):
        values = k_at(1, rt)

        def dk_step(b, acc, rt=rt, values=values):
            dw = lax.dot_general(values, q_at(1, b), NT, preferred_element_type=F32)
            ds = (dw * f_buf[rt, b]).astype(BF16)
            ds_buf[rt, b] = ds
            return acc + jnp.dot(ds, q_at(0, b), preferred_element_type=F32)

        acc = lax.fori_loop(*p_blocks(rt), dk_step, jnp.zeros((RT, HD), F32))
        put_keys_grad(1, rt, acc * (scale / ATT_DIV))
    send_a2(1)

    for b in range(NPB):
        acc = jnp.zeros((HD, PB), F32)
        for rt in range(NRT):
            lo, hi = p_blocks(rt)
            if lo <= b < hi:
                acc = acc + jnp.dot(k_at(0, rt).T, ds_buf[rt, b], preferred_element_type=F32)
        dq_buf[b * PB:(b + 1) * PB, :] = acc.T * (scale / ATT_DIV)

    dq_view = dq_buf.reshape(2, NM, 2, PADH, HD)
    xs[...] = dq_view[:, :, 1 - kap]
    swap = pltpu.make_async_remote_copy(
        src_ref=xs, dst_ref=xr, send_sem=ss_x, recv_sem=rs_x,
        device_id=(dp, m * 2 + 1 - kap), device_id_type=MESH)
    swap.start()
    send_b2(1)
    swap.wait_recv()
    for mm in range(NM):
        g2[2, mm] = (dq_view[:, mm, kap] + xr[:, mm]).astype(BF16)
    send_a2(2)
    send_b2(2)

    for g, out in ((0, ov_ref), (1, ok_ref), (2, oq_ref)):
        wait_b(sb2.at[g], rb2.at[g], g, ss_b2, rs_b2)
        for j in range(NDP):
            scr[j * HALF:(j + 1) * HALF, :] = rb2[g, j][:HALF].astype(F32)
        rows = jnp.concatenate(
            [scr[pl.ds(h, ROWS, stride=HEADS), :].astype(BF16) for h in range(HEADS)], axis=1)
        out[...] = jnp.dot(to_arrival, rows, preferred_element_type=F32).astype(BF16)

    drain_b(sb_qk, rb_qk, 0, ss_b, rs_b)
    drain_b(sb_1.at[0], rb_1.at[0], 1, ss_b, rs_b)
    drain_b(sb_1.at[1], rb_1.at[1], 2, ss_b, rs_b)
    for g in range(3):
        drain_b(sb2.at[g], rb2.at[g], g, ss_b2, rs_b2)

    def drain_m(e, c):
        for arr in range(4):
            copy_a(arr, m_peer(e)).wait_send()
        for g in range(3):
            copy_a2(g, m_peer(e)).wait_send()
        return c

    lax.fori_loop(1, NM, drain_m, 0)

    def drain_f(e, c):
        for a in range(2):
            copy_f(a, e, kap).wait_send()
        return c

    lax.fori_loop(0, NM, drain_f, 0)
    swap.wait_send()


def local(queries, keys, values, gates, attn_out, grad_out, route, lengths):
    vmem = pl.BlockSpec(memory_space=pltpu.VMEM)
    smem = pl.BlockSpec(memory_space=pltpu.SMEM)
    dma = pltpu.SemaphoreType.DMA
    shape = jax.ShapeDtypeStruct((ROWS, D), BF16)
    outs = pl.pallas_call(
        kernel,
        name="hstu_backward",
        out_shape=[shape] * 4,
        in_specs=[smem] * 2 + [vmem] * 6,
        out_specs=[vmem] * 4,
        scratch_shapes=[
            pltpu.VMEM((ROWS * 16, HD), F32),
            pltpu.VMEM((NDP, ROWS, HD), BF16),
            pltpu.VMEM((NDP, ROWS, HD), BF16),
            pltpu.VMEM((2, NDP, PADH, HD), BF16),
            pltpu.VMEM((2, NDP, PADH, HD), BF16),
            pltpu.VMEM((4, NM, 2, PADH, HD), BF16),
            pltpu.VMEM((2, 2, NCTX, PADH, HD), BF16),
            pltpu.VMEM((2, 2, NM, PADH, HD), BF16),
            pltpu.VMEM((NRT, NPB, RT, PB), BF16),
            pltpu.VMEM((NRT, NPB, RT, PB), F32),
            pltpu.VMEM((NRT, NPB, RT, PB), BF16),
            pltpu.VMEM((NPB * PB, HD), F32),
            pltpu.VMEM((2, NM, PADH, HD), F32),
            pltpu.VMEM((2, NM, PADH, HD), F32),
            pltpu.VMEM((3, NM, 2, PADH, HD), BF16),
            pltpu.VMEM((3, NM, 2, PADH, HD), BF16),
            pltpu.VMEM((3, NDP, PADH, HD), BF16),
            pltpu.VMEM((3, NDP, PADH, HD), BF16),
            dma((3, NDP)), dma((3, NDP)),
            dma((4, NM)), dma((4, NM)),
            dma((2, NM)), dma((2, NM)),
            dma, dma,
            dma((3, NM)), dma((3, NM)),
            dma((3, NDP)), dma((3, NDP)),
        ],
        compiler_params=pltpu.CompilerParams(
            collective_id=0, has_side_effects=True, vmem_limit_bytes=56 * 1024 * 1024
        ),
        cost_estimate=pl.CostEstimate(flops=3_400_000_000, bytes_accessed=3_000_000, transcendentals=2_000_000),
    )(route, lengths, queries[0], keys[0], values[0], gates[0], attn_out[0], grad_out[0])
    return tuple(x[None] for x in outs)


def solution(mesh):
    rows = P("dp", "ctx", None)
    return jax.shard_map(
        local,
        mesh=mesh,
        in_specs=(rows,) * 6 + (P("dp", "ctx"), P("dp", None)),
        out_specs=(rows,) * 4,
        check_vma=False,
    )
```

```python
import math

import jax
import jax.numpy as jnp
from jax import lax
from jax.experimental import pallas as pl
from jax.experimental.pallas import tpu as pltpu
from jax.sharding import PartitionSpec as P

D = 1024
HEADS = 8
HD = 128
ROWS = 144
HALF = 72
PADH = 80
BLK = 9
NDP = 16
NZ = 8
NCTX = 16
NM = 8
USERS = 4
ATT_DIV = 32
RT = 160
PB = 256
NRT = 8
NPB = 10
MESH = pl.DeviceIdType.MESH
F32 = jnp.float32
BF16 = jnp.bfloat16
NT = (((1,), (1,)), ((), ()))


def p_blocks(rt):
    return (rt, NPB) if rt < 4 else (5, 7 + rt - 4)


def kernel(
    tgt, lens, q_ref, k_ref, v_ref, u_ref, o_ref, dy_ref,
    oq_ref, ok_ref, ov_ref, ou_ref,
    held, done, scr, sb_qk, rb_qk, sb_1, rb_1, sa, qd, kv, w_buf, f_buf, ds_buf,
    dq_buf, xs, xr, g2, r2, sb2, rb2, at_query,
    in_sem, out_sem, ss_b, rs_b, ss_a, rs_a, ss_f, rs_f, ss_x, rs_x, ss_a2, rs_a2, ss_b2, rs_b2,
):
    dp = lax.axis_index("dp")
    ctx = lax.axis_index("ctx")
    xlo, z = dp // NZ, dp % NZ
    m, kap = ctx // 2, ctx % 2
    scale = 1.0 / math.sqrt(HD)

    def dp_peer(d):
        return ((xlo + d) % 2) * NZ + (z + d // 2) % NZ

    def m_peer(e):
        return (m + e) % NM

    loads = [
        pltpu.make_async_copy(ref, held.at[n], in_sem.at[n])
        for n, ref in enumerate((q_ref, k_ref, o_ref, dy_ref, u_ref, v_ref))
    ]
    for load in loads:
        load.start()

    barrier = pltpu.get_barrier_semaphore()

    def greet_dp(d, c):
        pl.semaphore_signal(barrier, inc=1, device_id=(dp_peer(d), ctx), device_id_type=MESH)
        return c

    def greet_m(e, c):
        pl.semaphore_signal(barrier, inc=1, device_id=(dp, m_peer(e) * 2 + kap), device_id_type=MESH)
        return c

    lax.fori_loop(1, NDP, greet_dp, 0)
    lax.fori_loop(1, NM, greet_m, 0)
    pl.semaphore_signal(barrier, inc=1, device_id=(dp, m * 2 + 1 - kap), device_id_type=MESH)

    row = lax.broadcasted_iota(jnp.int32, (ROWS, ROWS), 0)
    col = lax.broadcasted_iota(jnp.int32, (ROWS, ROWS), 1)
    shift_c = jnp.zeros((ROWS, ROWS), jnp.int32)
    shift_r = jnp.zeros((ROWS, ROWS), jnp.int32)
    for b in range(NDP):
        by = (tgt[0, b] - b) * BLK
        shift_c = jnp.where((col >= b * BLK) & (col < b * BLK + BLK), by, shift_c)
        shift_r = jnp.where((row >= b * BLK) & (row < b * BLK + BLK), by, shift_r)
    to_stream = jnp.where(row == col + shift_c, 1.0, 0.0).astype(BF16)
    to_arrival = jnp.where(col == row + shift_r, 1.0, 0.0).astype(BF16)

    drains = []

    def pack_b(arrays, dst):
        n = len(arrays) * HEADS
        for a, x in enumerate(arrays):
            y = jnp.dot(to_stream, x, preferred_element_type=F32)
            for h in range(HEADS):
                scr[pl.ds(a * HEADS + h, ROWS, stride=n), :] = y[:, h * HD:(h + 1) * HD]
        size = dst.shape[1]
        for j in range(NDP):
            dst[j] = scr[j * BLK * n:j * BLK * n + size, :].astype(BF16)

    def copy_b(src, dst, ch, peer, ssem, rsem):
        return pltpu.make_async_remote_copy(
            src_ref=src.at[peer], dst_ref=dst.at[dp], send_sem=ssem.at[ch, peer], recv_sem=rsem.at[ch, dp],
            device_id=(peer, ctx), device_id_type=MESH)

    def arrival_b(src, dst, ch, peer, ssem, rsem):
        return pltpu.make_async_remote_copy(
            src_ref=src.at[peer], dst_ref=dst.at[peer], send_sem=ssem.at[ch, peer], recv_sem=rsem.at[ch, peer],
            device_id=(peer, ctx), device_id_type=MESH)

    def send_b(src, dst, ch, ssem, rsem):
        def step(d, c):
            copy_b(src, dst, ch, dp_peer(d), ssem, rsem).start()
            return c

        lax.fori_loop(1, NDP, step, 0)
        dst[dp] = src[dp]
        drains.append(lambda: drain_b(src, dst, ch, ssem, rsem))

    def wait_b(src, dst, ch, ssem, rsem):
        def step(d, c):
            arrival_b(src, dst, ch, dp_peer(d), ssem, rsem).wait_recv()
            return c

        lax.fori_loop(1, NDP, step, 0)

    def drain_b(src, dst, ch, ssem, rsem):
        def step(d, c):
            copy_b(src, dst, ch, dp_peer(d), ssem, rsem).wait_send()
            return c

        lax.fori_loop(1, NDP, step, 0)

    zeros8 = jnp.zeros((PADH - HALF, HD), F32)

    def pack_a(src, arrays):
        n = len(arrays) * HEADS
        for i in range(NDP):
            scr[i * BLK * n:(i + 1) * BLK * n, :] = src[i][:BLK * n].astype(F32)
        for a, arr in enumerate(arrays):
            for h in range(HEADS):
                x = scr[pl.ds(a * HEADS + h, ROWS, stride=n), :]
                sa[arr, h, 0] = jnp.concatenate([x[:HALF], zeros8], axis=0).astype(BF16)
                sa[arr, h, 1] = jnp.concatenate([x[HALF:], zeros8], axis=0).astype(BF16)

    def slot_a(arr, mm):
        return qd.at[arr // 2, :, mm * 2 + kap] if arr % 2 == 0 else kv.at[arr // 2, :, mm]

    def copy_a(arr, peer):
        return pltpu.make_async_remote_copy(
            src_ref=sa.at[arr, peer], dst_ref=slot_a(arr, m), send_sem=ss_a.at[arr, peer], recv_sem=rs_a.at[arr, m],
            device_id=(dp, peer * 2 + kap), device_id_type=MESH)

    def arrival_a(arr, peer):
        return pltpu.make_async_remote_copy(
            src_ref=sa.at[arr, peer], dst_ref=slot_a(arr, peer), send_sem=ss_a.at[arr, peer], recv_sem=rs_a.at[arr, peer],
            device_id=(dp, peer * 2 + kap), device_id_type=MESH)

    def send_a(arr):
        def step(e, c):
            copy_a(arr, m_peer(e)).start()
            return c

        lax.fori_loop(1, NM, step, 0)
        if arr % 2 == 0:
            qd[arr // 2, :, ctx] = sa[arr, m]
        else:
            kv[arr // 2, :, m] = sa[arr, m]
        drains.append(lambda: drain_m(copy_a, arr))

    def drain_m(copy, n):
        def step(e, c):
            copy(n, m_peer(e)).wait_send()
            return c

        lax.fori_loop(1, NM, step, 0)

    def copy_f(a, mm, par):
        ref = qd.at[a, :, mm * 2 + par]
        return pltpu.make_async_remote_copy(
            src_ref=ref, dst_ref=ref, send_sem=ss_f.at[a, mm], recv_sem=rs_f.at[a, mm],
            device_id=(dp, m * 2 + 1 - kap), device_id_type=MESH)

    def wait_a(arr):
        def step(e, c):
            arrival_a(arr, m_peer(e)).wait_recv()
            if arr % 2 == 0:
                copy_f(arr // 2, m_peer(e), kap).start()
            return c

        if arr % 2 == 0:
            copy_f(arr // 2, m, kap).start()
            drains.append(lambda: drain_f(arr // 2))
        lax.fori_loop(1, NM, step, 0)

    def drain_f(a):
        def step(e, c):
            copy_f(a, e, kap).wait_send()
            return c

        lax.fori_loop(0, NM, step, 0)

    def wait_f(a):
        def step(e, c):
            copy_f(a, m_peer(e), 1 - kap).wait_recv()
            return c

        lax.fori_loop(0, NM, step, 0)

    loads[0].wait()
    loads[1].wait()
    pack_b([held[0], held[1]], sb_qk)
    pl.semaphore_wait(barrier, NDP - 1 + NM - 1 + 1)
    send_b(sb_qk, rb_qk, 0, ss_b, rs_b)

    for load in loads[2:5]:
        load.wait()
    o_full = held[2].astype(F32)
    centred = o_full - jnp.mean(o_full, axis=1, keepdims=True)
    inv_std = 1.0 / jnp.sqrt(jnp.mean(centred * centred, axis=1, keepdims=True) + 1e-05)
    normed = centred * inv_std
    dy_full = held[3].astype(F32)
    done[3] = (dy_full * normed).astype(BF16)
    store_u = pltpu.make_async_copy(done.at[3], ou_ref, out_sem.at[3])
    store_u.start()
    drains.append(store_u.wait)
    g_term = dy_full * held[4].astype(F32)
    d_o = inv_std * (
        g_term
        - jnp.mean(g_term, axis=1, keepdims=True)
        - normed * jnp.mean(g_term * normed, axis=1, keepdims=True)
    )
    pack_b([d_o.astype(BF16)], sb_1.at[0])
    send_b(sb_1.at[0], rb_1.at[0], 1, ss_b, rs_b)
    loads[5].wait()
    pack_b([held[5]], sb_1.at[1])
    send_b(sb_1.at[1], rb_1.at[1], 2, ss_b, rs_b)

    ends = []
    total = jnp.int32(0)
    for user in range(USERS):
        total = total + lens[0, user]
        ends.append(total)
    lane = lax.broadcasted_iota(jnp.int32, (8, NPB * PB), 1)
    late = lane >= NCTX * PADH
    lane_in = lane - jnp.where(late, NCTX * PADH, 0)
    chunk = jnp.zeros_like(lane_in)
    for c in range(1, NCTX):
        chunk = chunk + jnp.where(lane_in >= c * PADH, 1, 0)
    place = jnp.where(late, 2 * NCTX - 1 - chunk, chunk) * HALF + lane_in - chunk * PADH
    first = jnp.zeros_like(place)
    for user in range(USERS - 1):
        first = jnp.maximum(first, jnp.where(ends[user] <= place, ends[user], 0))
    at_query[0] = place
    at_query[1] = first

    sub = lax.broadcasted_iota(jnp.int32, (RT, PB), 0)
    second = jnp.where(sub >= PADH, 1, 0)

    def key_places(rt):
        c = 2 * (2 * (rt % 4) + second) + kap
        return (c if rt < 4 else 2 * NCTX - 1 - c) * HALF + sub - second * PADH

    def q_at(a, lo, hi):
        return qd.at[a].reshape(2 * NCTX * PADH, HD)[lo * PB:hi * PB, :]

    def k_at(a, rt):
        return kv.at[a].reshape(2 * NM * PADH, HD)[rt * RT:(rt + 1) * RT, :]

    wait_b(sb_qk, rb_qk, 0, ss_b, rs_b)
    pack_a(rb_qk, [0, 1])
    send_a(0)
    send_a(1)

    wait_b(sb_1.at[0], rb_1.at[0], 1, ss_b, rs_b)
    pack_a(rb_1.at[0], [2])
    send_a(2)

    wait_a(0)
    wait_a(1)
    wait_f(0)

    for rt in range(NRT):
        keys = k_at(0, rt)
        key_place = key_places(rt)

        for b in range(*p_blocks(rt)):
            at = slice(b * PB, (b + 1) * PB)
            s = lax.dot_general(keys, q_at(0, b, b + 1), NT, preferred_element_type=F32) * scale
            sig = 0.5 * jnp.tanh(0.5 * s) + 0.5
            live = (key_place <= at_query[0, :1, at]) & (key_place >= at_query[1, :1, at])
            sig = jnp.where(live, sig, 0.0)
            w = s * sig
            w_buf[rt, :, at] = w.astype(BF16)
            f_buf[rt, :, at] = sig * (1.0 - w) + w

    wait_b(sb_1.at[1], rb_1.at[1], 2, ss_b, rs_b)
    pack_a(rb_1.at[1], [3])
    send_a(3)

    wait_a(2)
    wait_f(1)

    def copy_a2(g, peer):
        return pltpu.make_async_remote_copy(
            src_ref=g2.at[g, peer], dst_ref=r2.at[g, m], send_sem=ss_a2.at[g, peer], recv_sem=rs_a2.at[g, m],
            device_id=(dp, peer * 2 + kap), device_id_type=MESH)

    def arrival_a2(g, peer):
        return pltpu.make_async_remote_copy(
            src_ref=g2.at[g, peer], dst_ref=r2.at[g, peer], send_sem=ss_a2.at[g, peer], recv_sem=rs_a2.at[g, peer],
            device_id=(dp, peer * 2 + kap), device_id_type=MESH)

    def send_a2(g):
        def step(e, c):
            copy_a2(g, m_peer(e)).start()
            return c

        lax.fori_loop(1, NM, step, 0)
        r2[g, m] = g2[g, m]
        drains.append(lambda: drain_m(copy_a2, g))

    def send_b2(g):
        def step(e, c):
            arrival_a2(g, m_peer(e)).wait_recv()
            return c

        lax.fori_loop(1, NM, step, 0)
        for h in range(HEADS):
            scr[pl.ds(h, HALF, stride=HEADS), :] = r2[g, h, 0].astype(F32)[:HALF]
            scr[pl.ds(HALF * HEADS + h, HALF, stride=HEADS), :] = r2[g, h, 1].astype(F32)[:HALF]
        for i in range(NDP):
            sb2[g, i] = scr[i * HALF:i * HALF + PADH, :].astype(BF16)
        send_b(sb2.at[g], rb2.at[g], g, ss_b2, rs_b2)

    def put_keys_grad(g, rt, value):
        t, half = rt % 4, rt // 4
        g2[g, 2 * t, half] = value[:PADH].astype(BF16)
        g2[g, 2 * t + 1, half] = value[PADH:].astype(BF16)

    for rt in range(NRT):
        lo, hi = p_blocks(rt)
        acc = jnp.dot(w_buf[rt, :, lo * PB:hi * PB], q_at(1, lo, hi), preferred_element_type=F32)
        put_keys_grad(0, rt, acc * (1.0 / ATT_DIV))
    send_a2(0)

    wait_a(3)

    for rt in range(NRT):
        values = k_at(1, rt)

        lo, hi = p_blocks(rt)
        for b in range(lo, hi):
            at = slice(b * PB, (b + 1) * PB)
            dw = lax.dot_general(values, q_at(1, b, b + 1), NT, preferred_element_type=F32)
            ds_buf[rt, :, at] = (dw * f_buf[rt, :, at]).astype(BF16)
        acc = jnp.dot(ds_buf[rt, :, lo * PB:hi * PB], q_at(0, lo, hi), preferred_element_type=F32)
        put_keys_grad(1, rt, acc * (scale / ATT_DIV))
    send_a2(1)
    send_b2(0)

    dq_view = dq_buf.reshape(2, NM, 2, PADH, HD)

    def swap(half):
        return pltpu.make_async_remote_copy(
            src_ref=xs.at[half], dst_ref=xr.at[half], send_sem=ss_x.at[half], recv_sem=rs_x.at[half],
            device_id=(dp, m * 2 + 1 - kap), device_id_type=MESH)

    for half in range(2):
        for b in range(half * NPB // 2, (half + 1) * NPB // 2):
            acc = jnp.zeros((HD, PB), F32)
            for rt in range(NRT):
                lo, hi = p_blocks(rt)
                if lo <= b < hi:
                    acc = acc + jnp.dot(
                        k_at(0, rt).T, ds_buf[rt, :, b * PB:(b + 1) * PB], preferred_element_type=F32)
            dq_buf[b * PB:(b + 1) * PB, :] = acc.T * (scale / ATT_DIV)
        xs[half] = dq_view[half, :, 1 - kap]
        swap(half).start()
        drains.append(swap(half).wait_send)
    for half in range(2):
        swap(half).wait_recv()
        for mm in range(NM):
            g2[2, mm, half] = (dq_view[half, mm, kap] + xr[half, mm]).astype(BF16)
    send_a2(2)
    send_b2(1)
    send_b2(2)

    for g, out in enumerate((ov_ref, ok_ref, oq_ref)):
        wait_b(sb2.at[g], rb2.at[g], g, ss_b2, rs_b2)
        for j in range(NDP):
            scr[j * HALF:(j + 1) * HALF, :] = rb2[g, j][:HALF].astype(F32)
        rows = jnp.concatenate(
            [scr[pl.ds(h, ROWS, stride=HEADS), :].astype(BF16) for h in range(HEADS)], axis=1)
        done[g] = jnp.dot(to_arrival, rows, preferred_element_type=F32).astype(BF16)
        store = pltpu.make_async_copy(done.at[g], out, out_sem.at[g])
        store.start()
        drains.append(store.wait)

    for drain in drains:
        drain()


def local(queries, keys, values, gates, attn_out, grad_out, route, lengths):
    hbm = pl.BlockSpec(memory_space=pl.ANY)
    smem = pl.BlockSpec(memory_space=pltpu.SMEM)
    dma = pltpu.SemaphoreType.DMA
    shape = jax.ShapeDtypeStruct((ROWS, D), BF16)
    outs = pl.pallas_call(
        kernel,
        name="hstu_backward",
        out_shape=[shape] * 4,
        in_specs=[smem] * 2 + [hbm] * 6,
        out_specs=[hbm] * 4,
        scratch_shapes=[
            pltpu.VMEM((6, ROWS, D), BF16),
            pltpu.VMEM((4, ROWS, D), BF16),
            pltpu.VMEM((ROWS * 16, HD), F32),
            pltpu.VMEM((NDP, ROWS, HD), BF16),
            pltpu.VMEM((NDP, ROWS, HD), BF16),
            pltpu.VMEM((2, NDP, PADH, HD), BF16),
            pltpu.VMEM((2, NDP, PADH, HD), BF16),
            pltpu.VMEM((4, NM, 2, PADH, HD), BF16),
            pltpu.VMEM((2, 2, NCTX, PADH, HD), BF16),
            pltpu.VMEM((2, 2, NM, PADH, HD), BF16),
            pltpu.VMEM((NRT, RT, NPB * PB), BF16),
            pltpu.VMEM((NRT, RT, NPB * PB), F32),
            pltpu.VMEM((NRT, RT, NPB * PB), BF16),
            pltpu.VMEM((NPB * PB, HD), F32),
            pltpu.VMEM((2, NM, PADH, HD), F32),
            pltpu.VMEM((2, NM, PADH, HD), F32),
            pltpu.VMEM((3, NM, 2, PADH, HD), BF16),
            pltpu.VMEM((3, NM, 2, PADH, HD), BF16),
            pltpu.VMEM((3, NDP, PADH, HD), BF16),
            pltpu.VMEM((3, NDP, PADH, HD), BF16),
            pltpu.VMEM((2, 8, NPB * PB), jnp.int32),
            dma((6,)), dma((4,)),
            dma((3, NDP)), dma((3, NDP)),
            dma((4, NM)), dma((4, NM)),
            dma((2, NM)), dma((2, NM)),
            dma((2,)), dma((2,)),
            dma((3, NM)), dma((3, NM)),
            dma((3, NDP)), dma((3, NDP)),
        ],
        compiler_params=pltpu.CompilerParams(
            collective_id=0, has_side_effects=True, vmem_limit_bytes=56 * 1024 * 1024
        ),
        cost_estimate=pl.CostEstimate(flops=3_400_000_000, bytes_accessed=3_000_000, transcendentals=2_000_000),
    )(route, lengths, queries[0], keys[0], values[0], gates[0], attn_out[0], grad_out[0])
    return tuple(x[None] for x in outs)


def solution(mesh):
    rows = P("dp", "ctx", None)
    return jax.shard_map(
        local,
        mesh=mesh,
        in_specs=(rows,) * 6 + (P("dp", "ctx"), P("dp", None)),
        out_specs=(rows,) * 4,
        check_vma=False,
    )
```

```python
import math

import jax
import jax.numpy as jnp
from jax import lax
from jax.experimental import pallas as pl
from jax.experimental.pallas import tpu as pltpu
from jax.sharding import PartitionSpec as P

D = 1024
HEADS = 8
HD = 128
ROWS = 144
HALF = 72
PADH = 80
BLK = 9
NDP = 16
NZ = 8
NCTX = 16
NM = 8
USERS = 4
ATT_DIV = 32
RT = 160
PB = 256
NRT = 8
NPB = 10
NXY = 16
NB = 2 * BLK * HEADS
MESH = pl.DeviceIdType.MESH
F32 = jnp.float32
BF16 = jnp.bfloat16
NT = (((1,), (1,)), ((), ()))

GROUPS = ((0, 4, 0, 32), (4, 9, 32, 80))
WHOLE = (0, PADH)
PARTS = ((0, 32), (32, 80))
B_PARTS = ((0, 64), (64, NB))


def p_blocks(rt):
    return (rt, NPB) if rt < 4 else (5, 7 + rt - 4)


def inner_place(x):
    y = x - 32
    block = (y * 205) // 1024
    return jnp.where(x < 32, (x // 4) * BLK + x % 4, block * BLK + 4 + y - 5 * block)


def one_hots(tgt):
    row = lax.broadcasted_iota(jnp.int32, (ROWS, ROWS), 0)
    col = lax.broadcasted_iota(jnp.int32, (ROWS, ROWS), 1)
    shift_c = jnp.zeros((ROWS, ROWS), jnp.int32)
    shift_r = jnp.zeros((ROWS, ROWS), jnp.int32)
    for b in range(NDP):
        by = (tgt[0, b] - b) * BLK
        shift_c = jnp.where((col >= b * BLK) & (col < b * BLK + BLK), by, shift_c)
        shift_r = jnp.where((row >= b * BLK) & (row < b * BLK + BLK), by, shift_r)
    to_stream = jnp.where(row == col + shift_c, 1.0, 0.0).astype(BF16)
    to_arrival = jnp.where(col == row + shift_r, 1.0, 0.0).astype(BF16)
    return to_stream, to_arrival


def unpack(blocks, scr, to_arrival):
    for other in range(NZ):
        x = blocks[other].astype(F32)
        for stream in range(2):
            at = (stream * NZ + other) * HALF
            scr[at:at + 32, :] = x[stream * 32:stream * 32 + 32]
            scr[at + 32:at + HALF, :] = x[64 + stream * 40:104 + stream * 40]
    rows = jnp.concatenate(
        [scr[pl.ds(h, ROWS, stride=HEADS), :].astype(BF16) for h in range(HEADS)], axis=1)
    return jnp.dot(to_arrival, rows, preferred_element_type=F32).astype(BF16)


def kernel(
    tgt, lens, q_ref, k_ref, v_ref, u_ref, o_ref, dy_ref,
    oq_ref, ok_ref, ov_ref, ou_ref,
    held, done, scr, sb, rb, sa, qd, kv, kt, w_buf, f_buf, ds_buf,
    dq_buf, xs, xr, g2, r2, sb2, rb2, at_query,
    in_sem, out_sem, sent, rs_b, rs_a, rs_f, rs_x, rs_a2, rs_b2,
):
    dp = lax.axis_index("dp")
    ctx = lax.axis_index("ctx")
    xlo, z = dp // NZ, dp % NZ
    m, kap = ctx // 2, ctx % 2
    scale = 1.0 / math.sqrt(HD)
    twin = (dp, m * 2 + 1 - kap)

    def z_peer(d):
        return (z + d) % NZ

    def at_z(other):
        return (xlo * NZ + other, ctx)

    def xy_peer(e):
        return ((xlo + e) % 2) * NM + (m + e // 2) % NM

    def at_xy(unit):
        return ((unit // NM) * NZ + z, (unit % NM) * 2 + kap)

    mine = xlo * NM + m

    def loop(lo, hi, body):
        def step(i, c):
            body(i)
            return c

        lax.fori_loop(lo, hi, step, 0)

    loads = [
        pltpu.make_async_copy(ref, held.at[n], in_sem.at[n])
        for n, ref in enumerate((q_ref, k_ref, o_ref, dy_ref, u_ref, v_ref))
    ]
    for load in loads:
        load.start()

    barrier = pltpu.get_barrier_semaphore()
    loop(1, NZ, lambda d: pl.semaphore_signal(
        barrier, inc=1, device_id=at_z(z_peer(d)), device_id_type=MESH))
    loop(1, NXY, lambda e: pl.semaphore_signal(
        barrier, inc=1, device_id=at_xy(xy_peer(e)), device_id_type=MESH))
    pl.semaphore_signal(barrier, inc=1, device_id=twin, device_id_type=MESH)

    to_stream, to_arrival = one_hots(tgt)

    def pack_b(arrays, lo):
        n = len(arrays) * HEADS
        for a, x in enumerate(arrays):
            y = jnp.dot(to_stream, x, preferred_element_type=F32)
            for h in range(HEADS):
                scr[pl.ds(a * HEADS + h, ROWS, stride=n), :] = y[:, h * HD:(h + 1) * HD]
        for other in range(NZ):
            pieces = []
            for first, last, _, _ in GROUPS:
                for stream in range(2):
                    at = (stream * NZ + other) * BLK * n
                    pieces.append(scr[at + first * n:at + last * n, :])
            sb[other, lo:lo + 2 * BLK * n] = jnp.concatenate(pieces, axis=0).astype(BF16)

    def send_b(src, dst, lo, hi, send_sem, recv_sem):
        rows = pl.ds(lo, hi - lo)

        def step(d):
            other = z_peer(d)
            pltpu.make_async_remote_copy(
                src_ref=src.at[other, rows], dst_ref=dst.at[z, rows], send_sem=send_sem, recv_sem=recv_sem,
                device_id=at_z(other), device_id_type=MESH).start()

        loop(1, NZ, step)

    def wait_b(src, dst, lo, hi, send_sem, recv_sem):
        part = (pl.ds(0, NZ - 1), pl.ds(lo, hi - lo))
        pltpu.make_async_remote_copy(
            src_ref=src.at[part], dst_ref=dst.at[part], send_sem=send_sem, recv_sem=recv_sem,
            device_id=at_z(z_peer(1)), device_id_type=MESH).wait_recv()

    zeros8 = jnp.zeros((8, HD), F32)

    def pack_a(lo, arrays, group):
        n = len(arrays) * HEADS
        first, last, at, end = group
        r = last - first
        base = lo + 2 * first * n
        for other in range(NZ):
            x = rb[other, base:base + 2 * r * n].astype(F32)
            for stream in range(2):
                at_scr = (stream * NZ + other) * r * n
                scr[at_scr:at_scr + r * n, :] = x[stream * r * n:(stream + 1) * r * n]
        for a, arr in enumerate(arrays):
            for h in range(HEADS):
                x = scr[pl.ds(a * HEADS + h, NDP * r, stride=n), :]
                for stream in range(2):
                    y = x[stream * 8 * r:(stream + 1) * 8 * r]
                    if end - at > 8 * r:
                        y = jnp.concatenate([y, zeros8], axis=0)
                    sa[arr, stream * NM + h, at:end] = y.astype(BF16)

    def slot_a(arr, rows):
        return qd.at[arr // 2, xlo, ctx, rows] if arr % 2 == 0 else kv.at[arr // 2, xlo, m, rows]

    def send_a(arr, lo, hi, recv_sem):
        rows = pl.ds(lo, hi - lo)

        def step(e):
            unit = xy_peer(e)
            pltpu.make_async_remote_copy(
                src_ref=sa.at[arr, unit, rows], dst_ref=slot_a(arr, rows), send_sem=sent.at[1], recv_sem=recv_sem,
                device_id=at_xy(unit), device_id_type=MESH).start()

        loop(1, NXY, step)
        if arr % 2 == 0:
            qd[arr // 2, xlo, ctx, rows] = sa[arr, mine, rows]
        else:
            kv[arr // 2, xlo, m, rows] = sa[arr, mine, rows]

    def wait_a(arr, lo, hi, recv_sem):
        part = sa.at[arr, pl.ds(0, NXY - 1), pl.ds(lo, hi - lo)]
        pltpu.make_async_remote_copy(
            src_ref=part, dst_ref=part, send_sem=sent.at[1], recv_sem=recv_sem,
            device_id=at_xy(xy_peer(1)), device_id_type=MESH).wait_recv()

    def share(a):
        def step(mm):
            ref = qd.at[a, :, mm * 2 + kap]
            pltpu.make_async_remote_copy(
                src_ref=ref, dst_ref=ref, send_sem=sent.at[2], recv_sem=rs_f.at[a],
                device_id=twin, device_id_type=MESH).start()

        loop(0, NM, step)

    def wait_share(a):
        part = qd.at[a, :, pl.ds(0, NM)]
        pltpu.make_async_remote_copy(
            src_ref=part, dst_ref=part, send_sem=sent.at[2], recv_sem=rs_f.at[a],
            device_id=twin, device_id_type=MESH).wait_recv()

    def send_a2(g, lo, hi, recv_sem):
        rows = pl.ds(lo, hi - lo)

        def step(e):
            unit = xy_peer(e)
            pltpu.make_async_remote_copy(
                src_ref=g2.at[g, unit, rows], dst_ref=r2.at[g, mine, rows], send_sem=sent.at[4], recv_sem=recv_sem,
                device_id=at_xy(unit), device_id_type=MESH).start()

        loop(1, NXY, step)
        r2[g, mine, rows] = g2[g, mine, rows]

    def send_b2(g, lo, hi, from_sem, dst, recv_sem):
        part = r2.at[g, pl.ds(0, NXY - 1), pl.ds(lo, hi - lo)]
        pltpu.make_async_remote_copy(
            src_ref=part, dst_ref=part, send_sem=sent.at[4], recv_sem=from_sem,
            device_id=at_xy(xy_peer(1)), device_id_type=MESH).wait_recv()
        for first, last, at, end in GROUPS:
            if lo <= at < hi:
                r = last - first
                n = r * HEADS
                for stream in range(2):
                    for h in range(HEADS):
                        scr[pl.ds(stream * NZ * n + h, 8 * r, stride=HEADS), :] = (
                            r2[g, stream * NM + h, at:end].astype(F32)[:8 * r])
                for other in range(NZ):
                    sb2[g, other, 2 * at:2 * at + 2 * n] = jnp.concatenate(
                        [scr[(stream * NZ + other) * n:(stream * NZ + other + 1) * n, :] for stream in range(2)],
                        axis=0).astype(BF16)
        low, high = 2 * lo, min(2 * hi, NB)
        send_b(sb2.at[g], dst, low, high, sent.at[5], recv_sem)

    loads[0].wait()
    loads[1].wait()
    pack_b([held[0], held[1]], 0)
    pl.semaphore_wait(barrier, NZ - 1 + NXY - 1 + 1)
    b_qk = (sb, rb, 0, 2 * NB, sent.at[0], rs_b.at[0])
    send_b(*b_qk)
    rb[z, :2 * NB] = sb[z, :2 * NB]

    for load in loads[2:5]:
        load.wait()
    o_full = held[2].astype(F32)
    centred = o_full - jnp.mean(o_full, axis=1, keepdims=True)
    inv_std = 1.0 / jnp.sqrt(jnp.mean(centred * centred, axis=1, keepdims=True) + 1e-05)
    normed = centred * inv_std
    dy_full = held[3].astype(F32)
    done[3] = (dy_full * normed).astype(BF16)
    stores = [pltpu.make_async_copy(done.at[3], ou_ref, out_sem.at[3])]
    stores[0].start()
    g_term = dy_full * held[4].astype(F32)
    d_o = inv_std * (
        g_term
        - jnp.mean(g_term, axis=1, keepdims=True)
        - normed * jnp.mean(g_term * normed, axis=1, keepdims=True)
    )
    at_do, at_v = 2 * NB, 3 * NB
    pack_b([d_o.astype(BF16)], at_do)
    b_do = (sb, rb, at_do, at_do + NB, sent.at[0], rs_b.at[1])
    send_b(*b_do)
    loads[5].wait()
    pack_b([held[5]], at_v)
    b_v = [(sb, rb, at_v + lo, at_v + hi, sent.at[0], rs_b.at[2 + n]) for n, (lo, hi) in enumerate(B_PARTS)]
    for part in b_v:
        send_b(*part)
    rb[z, at_do:] = sb[z, at_do:]

    ends = []
    total = jnp.int32(0)
    for user in range(USERS):
        total = total + lens[0, user]
        ends.append(total)
    lane = lax.broadcasted_iota(jnp.int32, (8, NPB * PB), 1)
    late = lane >= NCTX * PADH
    lane_in = lane - jnp.where(late, NCTX * PADH, 0)
    chunk = jnp.zeros_like(lane_in)
    for c in range(1, NCTX):
        chunk = chunk + jnp.where(lane_in >= c * PADH, 1, 0)
    place = jnp.where(late, 2 * NCTX - 1 - chunk, chunk) * HALF + inner_place(lane_in - chunk * PADH)
    first = jnp.zeros_like(place)
    for user in range(USERS - 1):
        first = jnp.maximum(first, jnp.where(ends[user] <= place, ends[user], 0))
    at_query[0] = place
    at_query[1] = first

    sub = lax.broadcasted_iota(jnp.int32, (RT, PB), 0)
    second = jnp.where(sub >= PADH, 1, 0)
    key_inner = inner_place(sub - second * PADH)

    def key_places(rt):
        c = 2 * (2 * (rt % 4) + second) + kap
        return (c if rt < 4 else 2 * NCTX - 1 - c) * HALF + key_inner

    def q_at(a, lo, hi):
        return qd.at[a].reshape(2 * NCTX * PADH, HD)[lo * PB:hi * PB, :]

    def k_at(a, rt):
        return kv.at[a].reshape(2 * NM * PADH, HD)[rt * RT:(rt + 1) * RT, :]

    wait_b(*b_qk)
    for group in GROUPS:
        pack_a(0, [0, 1], group)
    send_a(0, *WHOLE, rs_a.at[0])
    send_a(1, *WHOLE, rs_a.at[1])

    wait_b(*b_do)
    for group in GROUPS:
        pack_a(at_do, [2], group)
    send_a(2, *WHOLE, rs_a.at[2])
    wait_a(0, *WHOLE, rs_a.at[0])
    share(0)

    wait_b(*b_v[0])
    pack_a(at_v, [3], GROUPS[0])
    send_a(3, *PARTS[0], rs_a.at[3])

    wait_b(*b_v[1])
    pack_a(at_v, [3], GROUPS[1])
    send_a(3, *PARTS[1], rs_a.at[4])

    wait_a(1, *WHOLE, rs_a.at[1])
    wait_share(0)

    for rt in range(NRT):
        keys = k_at(0, rt)
        kt[rt] = keys.T
        key_place = key_places(rt)
        for b in range(*p_blocks(rt)):
            at = slice(b * PB, (b + 1) * PB)
            s = lax.dot_general(keys, q_at(0, b, b + 1), NT, preferred_element_type=F32) * scale
            sig = 0.5 * jnp.tanh(0.5 * s) + 0.5
            live = (key_place <= at_query[0, :1, at]) & (key_place >= at_query[1, :1, at])
            sig = jnp.where(live, sig, 0.0)
            w = s * sig
            w_buf[rt, :, at] = w.astype(BF16)
            f_buf[rt, :, at] = sig * (1.0 - w) + w

    wait_a(2, *WHOLE, rs_a.at[2])
    share(1)
    wait_share(1)

    def put_keys_grad(g, rt, value):
        t, half = rt % 4, rt // 4
        g2[g, half * NM + 2 * t] = value[:PADH].astype(BF16)
        g2[g, half * NM + 2 * t + 1] = value[PADH:].astype(BF16)

    for rt in range(NRT):
        lo, hi = p_blocks(rt)
        acc = jnp.dot(w_buf[rt, :, lo * PB:hi * PB], q_at(1, lo, hi), preferred_element_type=F32)
        put_keys_grad(0, rt, acc * (1.0 / ATT_DIV))
    for n, part in enumerate(PARTS):
        send_a2(0, *part, rs_a2.at[n])

    for n, part in enumerate(PARTS):
        wait_a(3, *part, rs_a.at[3 + n])
    for rt in range(NRT):
        values = k_at(1, rt)
        lo, hi = p_blocks(rt)
        for b in range(lo, hi):
            at = slice(b * PB, (b + 1) * PB)
            dw = lax.dot_general(values, q_at(1, b, b + 1), NT, preferred_element_type=F32)
            ds_buf[rt, :, at] = (dw * f_buf[rt, :, at]).astype(BF16)
        acc = jnp.dot(ds_buf[rt, :, lo * PB:hi * PB], q_at(0, lo, hi), preferred_element_type=F32)
        put_keys_grad(1, rt, acc * (scale / ATT_DIV))
    send_a2(1, *WHOLE, rs_a2.at[2])
    for n, part in enumerate(PARTS):
        send_b2(0, *part, rs_a2.at[n], rb2.at[0], rs_b2.at[n])
    rb2[0, z] = sb2[0, z]

    dq_view = dq_buf.reshape(2, NM, 2, PADH, HD)

    def swap(half):
        return pltpu.make_async_remote_copy(
            src_ref=xs.at[half], dst_ref=xr.at[half], send_sem=sent.at[3], recv_sem=rs_x.at[half],
            device_id=twin, device_id_type=MESH)

    for half in range(2):
        for b in range(half * NPB // 2, (half + 1) * NPB // 2):
            acc = jnp.zeros((HD, PB), F32)
            for rt in range(NRT):
                lo, hi = p_blocks(rt)
                if lo <= b < hi:
                    acc = acc + jnp.dot(
                        kt[rt], ds_buf[rt, :, b * PB:(b + 1) * PB], preferred_element_type=F32)
            dq_buf[b * PB:(b + 1) * PB, :] = acc.T * (scale / ATT_DIV)
        xs[half] = dq_view[half, :, 1 - kap]
        swap(half).start()
    for half in range(2):
        swap(half).wait_recv()
        for mm in range(NM):
            g2[2, half * NM + mm] = (dq_view[half, mm, kap] + xr[half, mm]).astype(BF16)
    send_a2(2, *WHOLE, rs_a2.at[3])
    send_b2(1, *WHOLE, rs_a2.at[2], rb2.at[1], rs_b2.at[2])
    rb2[1, z] = sb2[1, z]
    send_b2(2, *WHOLE, rs_a2.at[3], oq_ref, rs_b2.at[3])
    keep = pltpu.make_async_copy(sb2.at[2, z], oq_ref.at[z], out_sem.at[2])
    keep.start()
    stores.append(keep)

    homes = (
        [(sb2.at[0], rb2.at[0], *part, sent.at[5], rs_b2.at[n]) for n, part in enumerate(B_PARTS)],
        [(sb2.at[1], rb2.at[1], 0, NB, sent.at[5], rs_b2.at[2])],
    )
    for g, out in enumerate((ov_ref, ok_ref)):
        for home in homes[g]:
            wait_b(*home)
        done[g] = unpack(rb2.at[g], scr, to_arrival)
        stores.append(pltpu.make_async_copy(done.at[g], out, out_sem.at[g]))
        stores[-1].start()
    wait_b(sb2.at[2], oq_ref, 0, NB, sent.at[5], rs_b2.at[3])

    for n, part in enumerate((
        sb.at[pl.ds(0, NZ - 1)], sa.at[:, pl.ds(0, NXY - 1)], qd.at[:, :, pl.ds(0, NM)], xs,
        g2.at[:, pl.ds(0, NXY - 1)], sb2.at[:, pl.ds(0, NZ - 1)],
    )):
        pltpu.make_async_remote_copy(
            src_ref=part, dst_ref=part, send_sem=sent.at[n], recv_sem=rs_x.at[0],
            device_id=twin, device_id_type=MESH).wait_send()
    for store in stores:
        store.wait()


def finish(tgt, q_ref, k_ref, v_ref, u_ref, oq_ref, ok_ref, ov_ref, ou_ref, blocks, rows, scr, sems):
    ins = [pltpu.make_async_copy(q_ref, blocks, sems.at[0])]
    outs = []
    for n, (ref, out) in enumerate(((k_ref, ok_ref), (v_ref, ov_ref), (u_ref, ou_ref))):
        ins.append(pltpu.make_async_copy(ref, rows.at[n], sems.at[n + 1]))
        outs.append(pltpu.make_async_copy(rows.at[n], out, sems.at[n + 4]))
    for copy in ins:
        copy.start()
    _, to_arrival = one_hots(tgt)
    ins[0].wait()
    rows[3] = unpack(blocks, scr, to_arrival)
    outs.append(pltpu.make_async_copy(rows.at[3], oq_ref, sems.at[7]))
    outs[3].start()
    for n in range(3):
        ins[n + 1].wait()
        outs[n].start()
    for copy in outs:
        copy.wait()


def local(queries, keys, values, gates, attn_out, grad_out, route, lengths):
    hbm = pl.BlockSpec(memory_space=pl.ANY)
    smem = pl.BlockSpec(memory_space=pltpu.SMEM)
    dma = pltpu.SemaphoreType.DMA
    shape = jax.ShapeDtypeStruct((ROWS, D), BF16)
    attention = (NRT, RT, NPB * PB)
    outs = pl.pallas_call(
        kernel,
        name="hstu_backward",
        out_shape=[jax.ShapeDtypeStruct((NZ, NB, HD), BF16)] + [shape] * 3,
        in_specs=[smem] * 2 + [hbm] * 6,
        out_specs=[hbm] * 4,
        scratch_shapes=[
            pltpu.VMEM((6, ROWS, D), BF16),
            pltpu.VMEM((4, ROWS, D), BF16),
            pltpu.VMEM((ROWS * 16, HD), F32),
            pltpu.VMEM((NZ, 4 * NB, HD), BF16),
            pltpu.VMEM((NZ, 4 * NB, HD), BF16),
            pltpu.VMEM((4, NXY, PADH, HD), BF16),
            pltpu.VMEM((2, 2, NCTX, PADH, HD), BF16),
            pltpu.VMEM((2, 2, NM, PADH, HD), BF16),
            pltpu.VMEM((NRT, HD, RT), BF16),
            pltpu.VMEM(attention, BF16),
            pltpu.VMEM(attention, F32),
            pltpu.VMEM(attention, BF16),
            pltpu.VMEM((NPB * PB, HD), F32),
            pltpu.VMEM((2, NM, PADH, HD), F32),
            pltpu.VMEM((2, NM, PADH, HD), F32),
            pltpu.VMEM((3, NXY, PADH, HD), BF16),
            pltpu.VMEM((3, NXY, PADH, HD), BF16),
            pltpu.VMEM((3, NZ, NB, HD), BF16),
            pltpu.VMEM((2, NZ, NB, HD), BF16),
            pltpu.VMEM((2, 8, NPB * PB), jnp.int32),
            dma((6,)), dma((4,)), dma((6,)),
            dma((4,)), dma((5,)), dma((2,)), dma((2,)), dma((4,)), dma((4,)),
        ],
        compiler_params=pltpu.CompilerParams(
            collective_id=0, has_side_effects=True, vmem_limit_bytes=56 * 1024 * 1024
        ),
        cost_estimate=pl.CostEstimate(flops=3_400_000_000, bytes_accessed=3_000_000, transcendentals=2_000_000),
    )(route, lengths, queries[0], keys[0], values[0], gates[0], attn_out[0], grad_out[0])
    outs = pl.pallas_call(
        finish,
        name="finish",
        out_shape=[shape] * 4,
        in_specs=[smem] + [hbm] * 4,
        out_specs=[hbm] * 4,
        scratch_shapes=[
            pltpu.VMEM((NZ, NB, HD), BF16),
            pltpu.VMEM((4, ROWS, D), BF16),
            pltpu.VMEM((ROWS * HEADS, HD), F32),
            dma((8,)),
        ],
        compiler_params=pltpu.CompilerParams(vmem_limit_bytes=56 * 1024 * 1024),
    )(route, *outs)
    return tuple(x[None] for x in outs)


def solution(mesh):
    rows = P("dp", "ctx", None)
    return jax.shard_map(
        local,
        mesh=mesh,
        in_specs=(rows,) * 6 + (P("dp", "ctx"), P("dp", None)),
        out_specs=(rows,) * 4,
        check_vma=False,
    )
```

```python
import math

import jax
import jax.numpy as jnp
from jax import lax
from jax.experimental import pallas as pl
from jax.experimental.pallas import tpu as pltpu
from jax.sharding import PartitionSpec as P

D = 1024
HEADS = 8
HD = 128
ROWS = 144
HALF = 72
PADH = 80
BLK = 9
NDP = 16
NZ = 8
NCTX = 16
NM = 8
USERS = 4
ATT_DIV = 32
RT = 160
PB = 256
NRT = 8
NPB = 10
NXY = 16
NB = 2 * BLK * HEADS
MESH = pl.DeviceIdType.MESH
F32 = jnp.float32
BF16 = jnp.bfloat16
NT = (((1,), (1,)), ((), ()))

GROUPS = ((0, 4, 0, 32), (4, 9, 32, 80))
WHOLE = (0, PADH)
PARTS = ((0, 32), (32, 80))
B_PARTS = ((0, 64), (64, NB))
IN_ONE = (((0, PADH), (0, NB), GROUPS),)
IN_TWO = (((0, 32), (0, 64), GROUPS[:1]), ((32, PADH), (64, NB), GROUPS[1:]))
CUT_QK, CUT_DO, CUT_V, CUT_DV, CUT_DK, CUT_DQ = IN_TWO, IN_ONE, IN_TWO, IN_TWO, IN_ONE, IN_ONE


def p_blocks(rt):
    return (rt, NPB) if rt < 4 else (5, 7 + rt - 4)


def inner_place(x):
    y = x - 32
    block = (y * 205) // 1024
    return jnp.where(x < 32, (x // 4) * BLK + x % 4, block * BLK + 4 + y - 5 * block)


def one_hots(tgt):
    row = lax.broadcasted_iota(jnp.int32, (ROWS, ROWS), 0)
    col = lax.broadcasted_iota(jnp.int32, (ROWS, ROWS), 1)
    shift_c = jnp.zeros((ROWS, ROWS), jnp.int32)
    shift_r = jnp.zeros((ROWS, ROWS), jnp.int32)
    for b in range(NDP):
        by = (tgt[0, b] - b) * BLK
        shift_c = jnp.where((col >= b * BLK) & (col < b * BLK + BLK), by, shift_c)
        shift_r = jnp.where((row >= b * BLK) & (row < b * BLK + BLK), by, shift_r)
    to_stream = jnp.where(row == col + shift_c, 1.0, 0.0).astype(BF16)
    to_arrival = jnp.where(col == row + shift_r, 1.0, 0.0).astype(BF16)
    return to_stream, to_arrival


def unpack(blocks, scr, to_arrival):
    for other in range(NZ):
        x = blocks[other].astype(F32)
        for stream in range(2):
            at = (stream * NZ + other) * HALF
            scr[at:at + 32, :] = x[stream * 32:stream * 32 + 32]
            scr[at + 32:at + HALF, :] = x[64 + stream * 40:104 + stream * 40]
    rows = jnp.concatenate(
        [scr[pl.ds(h, ROWS, stride=HEADS), :].astype(BF16) for h in range(HEADS)], axis=1)
    return jnp.dot(to_arrival, rows, preferred_element_type=F32).astype(BF16)


def kernel(
    tgt, lens, q_ref, k_ref, v_ref, u_ref, o_ref, dy_ref,
    oq_ref, ok_ref, ov_ref, ou_ref,
    held, done, scr, sb, rb, sa, events, kt, w_buf, f_buf, ds_buf,
    dq_buf, xs, xr, g2, r2, sb2, rb2, at_query,
    in_sem, out_sem, sent, rs_b, rs_a, rs_f, rs_x, rs_a2, rs_b2,
):
    dp = lax.axis_index("dp")
    ctx = lax.axis_index("ctx")
    xlo, z = dp // NZ, dp % NZ
    m, kap = ctx // 2, ctx % 2
    scale = 1.0 / math.sqrt(HD)
    twin = (dp, m * 2 + 1 - kap)

    def z_peer(d):
        return lax.rem(z + d, NZ)

    def at_z(other):
        return (xlo * NZ + other, ctx)

    def xy_peer(e):
        return lax.rem(xlo + e, 2) * NM + lax.rem(m + lax.div(e, 2), NM)

    def at_xy(unit):
        return (lax.div(unit, NM) * NZ + z, lax.rem(unit, NM) * 2 + kap)

    mine = xlo * NM + m

    def loop(lo, hi, body):
        def step(i, c):
            body(i)
            return c

        lax.fori_loop(lo, hi, step, 0, unroll=True)

    loads = [
        pltpu.make_async_copy(ref, held.at[n], in_sem.at[n])
        for n, ref in enumerate((q_ref, k_ref, o_ref, dy_ref, u_ref, v_ref))
    ]
    for load in loads:
        load.start()

    barrier = pltpu.get_barrier_semaphore()
    loop(1, NZ, lambda d: pl.semaphore_signal(
        barrier, inc=1, device_id=at_z(z_peer(d)), device_id_type=MESH))
    loop(1, NXY, lambda e: pl.semaphore_signal(
        barrier, inc=1, device_id=at_xy(xy_peer(e)), device_id_type=MESH))
    pl.semaphore_signal(barrier, inc=1, device_id=twin, device_id_type=MESH)

    to_stream, to_arrival = one_hots(tgt)

    def pack_b(arrays, lo):
        n = len(arrays) * HEADS
        for a, x in enumerate(arrays):
            y = jnp.dot(to_stream, x, preferred_element_type=F32)
            for h in range(HEADS):
                scr[pl.ds(a * HEADS + h, ROWS, stride=n), :] = y[:, h * HD:(h + 1) * HD]
        for other in range(NZ):
            pieces = []
            for first, last, _, _ in GROUPS:
                for stream in range(2):
                    at = (stream * NZ + other) * BLK * n
                    pieces.append(scr[at + first * n:at + last * n, :])
            sb[other, lo:lo + 2 * BLK * n] = jnp.concatenate(pieces, axis=0).astype(BF16)

    def send_b(src, dst, lo, hi, send_sem, recv_sem):
        rows = pl.ds(lo, hi - lo)

        def step(d):
            other = z_peer(d)
            pltpu.make_async_remote_copy(
                src_ref=src.at[other, rows], dst_ref=dst.at[z, rows], send_sem=send_sem, recv_sem=recv_sem,
                device_id=at_z(other), device_id_type=MESH).start()

        loop(1, NZ, step)

    def wait_b(src, dst, lo, hi, send_sem, recv_sem):
        part = (pl.ds(0, NZ - 1), pl.ds(lo, hi - lo))
        pltpu.make_async_remote_copy(
            src_ref=src.at[part], dst_ref=dst.at[part], send_sem=send_sem, recv_sem=recv_sem,
            device_id=at_z(z_peer(1)), device_id_type=MESH).wait_recv()

    zeros8 = jnp.zeros((8, HD), F32)

    def pack_a(lo, arrays, group):
        n = len(arrays) * HEADS
        first, last, at, end = group
        r = last - first
        base = lo + 2 * first * n
        for other in range(NZ):
            x = rb[other, base:base + 2 * r * n].astype(F32)
            for stream in range(2):
                at_scr = (stream * NZ + other) * r * n
                scr[at_scr:at_scr + r * n, :] = x[stream * r * n:(stream + 1) * r * n]
        for a, arr in enumerate(arrays):
            for h in range(HEADS):
                x = scr[pl.ds(a * HEADS + h, NDP * r, stride=n), :]
                for stream in range(2):
                    y = x[stream * 8 * r:(stream + 1) * 8 * r]
                    if end - at > 8 * r:
                        y = jnp.concatenate([y, zeros8], axis=0)
                    sa[arr, stream * NM + h, at:end] = y.astype(BF16)

    def send_a(arr, n, lo, hi, recv_sem):
        arrs, rows = pl.ds(arr, n), pl.ds(lo, hi - lo)

        def step(e):
            unit = xy_peer(e)
            pltpu.make_async_remote_copy(
                src_ref=sa.at[arrs, unit, rows], dst_ref=events.at[arrs, xlo, m, kap, rows],
                send_sem=sent.at[1], recv_sem=recv_sem, device_id=at_xy(unit), device_id_type=MESH).start()

        loop(1, NXY, step)
        events[arrs, xlo, m, kap, rows] = sa[arrs, mine, rows]

    def wait_a(arr, n, lo, hi, recv_sem):
        part = sa.at[pl.ds(arr, n), pl.ds(0, NXY - 1), pl.ds(lo, hi - lo)]
        pltpu.make_async_remote_copy(
            src_ref=part, dst_ref=part, send_sem=sent.at[1], recv_sem=recv_sem,
            device_id=at_xy(xy_peer(jnp.int32(1))), device_id_type=MESH).wait_recv()

    def share(arr, par, lo, hi, recv_sem):
        ref = events.at[arr, :, :, par, pl.ds(lo, hi - lo)]
        return pltpu.make_async_remote_copy(
            src_ref=ref, dst_ref=ref, send_sem=sent.at[2], recv_sem=recv_sem,
            device_id=twin, device_id_type=MESH)

    def send_a2(g, lo, hi, recv_sem):
        rows = pl.ds(lo, hi - lo)

        def step(e):
            unit = xy_peer(e)
            pltpu.make_async_remote_copy(
                src_ref=g2.at[g, unit, rows], dst_ref=r2.at[g, mine, rows], send_sem=sent.at[4], recv_sem=recv_sem,
                device_id=at_xy(unit), device_id_type=MESH).start()

        loop(1, NXY, step)
        r2[g, mine, rows] = g2[g, mine, rows]

    def send_b2(g, lo, hi, from_sem, dst, recv_sem):
        part = r2.at[g, pl.ds(0, NXY - 1), pl.ds(lo, hi - lo)]
        pltpu.make_async_remote_copy(
            src_ref=part, dst_ref=part, send_sem=sent.at[4], recv_sem=from_sem,
            device_id=at_xy(xy_peer(jnp.int32(1))), device_id_type=MESH).wait_recv()
        for first, last, at, end in GROUPS:
            if lo <= at < hi:
                r = last - first
                n = r * HEADS
                for stream in range(2):
                    for h in range(HEADS):
                        scr[pl.ds(stream * NZ * n + h, 8 * r, stride=HEADS), :] = (
                            r2[g, stream * NM + h, at:end].astype(F32)[:8 * r])
                for other in range(NZ):
                    sb2[g, other, 2 * at:2 * at + 2 * n] = jnp.concatenate(
                        [scr[(stream * NZ + other) * n:(stream * NZ + other + 1) * n, :] for stream in range(2)],
                        axis=0).astype(BF16)
        low, high = 2 * lo, min(2 * hi, NB)
        send_b(sb2.at[g], dst, low, high, sent.at[5], recv_sem)

    loads[0].wait()
    loads[1].wait()
    pack_b([held[0], held[1]], 0)
    pl.semaphore_wait(barrier, NZ - 1 + NXY - 1 + 1)
    b_qk = [(sb, rb, 2 * lo, 2 * hi, sent.at[0], rs_b.at[n]) for n, (_, (lo, hi), _) in enumerate(CUT_QK)]
    for part in b_qk:
        send_b(*part)
    rb[z, :2 * NB] = sb[z, :2 * NB]

    for load in loads[2:5]:
        load.wait()
    o_full = held[2].astype(F32)
    centred = o_full - jnp.mean(o_full, axis=1, keepdims=True)
    inv_std = 1.0 / jnp.sqrt(jnp.mean(centred * centred, axis=1, keepdims=True) + 1e-05)
    normed = centred * inv_std
    dy_full = held[3].astype(F32)
    done[3] = (dy_full * normed).astype(BF16)
    stores = [pltpu.make_async_copy(done.at[3], ou_ref, out_sem.at[3])]
    stores[0].start()
    g_term = dy_full * held[4].astype(F32)
    d_o = inv_std * (
        g_term
        - jnp.mean(g_term, axis=1, keepdims=True)
        - normed * jnp.mean(g_term * normed, axis=1, keepdims=True)
    )
    at_do, at_v = 2 * NB, 3 * NB
    pack_b([d_o.astype(BF16)], at_do)
    b_do = [(sb, rb, at_do + lo, at_do + hi, sent.at[0], rs_b.at[2 + n]) for n, (_, (lo, hi), _) in enumerate(CUT_DO)]
    for part in b_do:
        send_b(*part)
    loads[5].wait()
    pack_b([held[5]], at_v)
    b_v = [(sb, rb, at_v + lo, at_v + hi, sent.at[0], rs_b.at[4 + n]) for n, (_, (lo, hi), _) in enumerate(CUT_V)]
    for part in b_v:
        send_b(*part)
    rb[z, at_do:] = sb[z, at_do:]

    ends = []
    total = jnp.int32(0)
    for user in range(USERS):
        total = total + lens[0, user]
        ends.append(total)
    lane = lax.broadcasted_iota(jnp.int32, (8, NPB * PB), 1)
    late = lane >= NCTX * PADH
    lane_in = lane - jnp.where(late, NCTX * PADH, 0)
    chunk = jnp.zeros_like(lane_in)
    for c in range(1, NCTX):
        chunk = chunk + jnp.where(lane_in >= c * PADH, 1, 0)
    place = jnp.where(late, 2 * NCTX - 1 - chunk, chunk) * HALF + inner_place(lane_in - chunk * PADH)
    first = jnp.zeros_like(place)
    for user in range(USERS - 1):
        first = jnp.maximum(first, jnp.where(ends[user] <= place, ends[user], 0))
    at_query[0] = place
    at_query[1] = first

    sub = lax.broadcasted_iota(jnp.int32, (RT, PB), 0)
    second = jnp.where(sub >= PADH, 1, 0)
    key_inner = inner_place(sub - second * PADH)

    def key_places(rt):
        c = 2 * (2 * (rt % 4) + second) + kap
        return (c if rt < 4 else 2 * NCTX - 1 - c) * HALF + key_inner

    def q_at(a, lo, hi):
        return events.at[2 * a].reshape(2 * NCTX * PADH, HD)[lo * PB:hi * PB, :]

    def k_at(a, rt):
        half, t = rt // 4, rt % 4
        return jnp.concatenate([events[2 * a + 1, half, 2 * t + n, kap] for n in range(2)], axis=0)

    def get_b(parts, cut, n, lo, arrays):
        rows, _, groups = cut[n]
        wait_b(*parts[n])
        for group in groups:
            pack_a(lo, arrays, group)
        send_a(arrays[0], len(arrays), *rows, rs_a.at[arrays[0], n])

    def get_a(arr, count, cut):
        for n, (rows, _, _) in enumerate(cut):
            wait_a(arr, count, *rows, rs_a.at[arr, n])
            if arr < 3:
                share(arr, kap, *rows, rs_f.at[arr, n]).start()

    def get_share(arr, cut):
        for n, (rows, _, _) in enumerate(cut):
            share(arr, 1 - kap, *rows, rs_f.at[arr, n]).wait_recv()

    for n in range(len(CUT_QK)):
        get_b(b_qk, CUT_QK, n, 0, [0, 1])
    for n in range(len(CUT_DO)):
        get_b(b_do, CUT_DO, n, at_do, [2])
    get_a(0, 2, CUT_QK)
    get_share(0, CUT_QK)

    for rt in range(NRT):
        keys = k_at(0, rt)
        kt[rt] = keys.T
        key_place = key_places(rt)
        for b in range(*p_blocks(rt)):
            at = slice(b * PB, (b + 1) * PB)
            s = lax.dot_general(keys, q_at(0, b, b + 1), NT, preferred_element_type=F32) * scale
            sig = 0.5 * jnp.tanh(0.5 * s) + 0.5
            live = (key_place <= at_query[0, :1, at]) & (key_place >= at_query[1, :1, at])
            sig = jnp.where(live, sig, 0.0)
            w = s * sig
            w_buf[rt, :, at] = w.astype(BF16)
            f_buf[rt, :, at] = sig * (1.0 - w) + w

    get_b(b_v, CUT_V, 0, at_v, [3])
    get_a(2, 1, CUT_DO)
    get_b(b_v, CUT_V, 1, at_v, [3])
    get_share(2, CUT_DO)

    def put_keys_grad(g, rt, value):
        t, half = rt % 4, rt // 4
        g2[g, half * NM + 2 * t] = value[:PADH].astype(BF16)
        g2[g, half * NM + 2 * t + 1] = value[PADH:].astype(BF16)

    for rt in range(NRT):
        lo, hi = p_blocks(rt)
        acc = jnp.dot(w_buf[rt, :, lo * PB:hi * PB], q_at(1, lo, hi), preferred_element_type=F32)
        put_keys_grad(0, rt, acc * (1.0 / ATT_DIV))
    for n, (rows, _, _) in enumerate(CUT_DV):
        send_a2(0, *rows, rs_a2.at[0, n])

    get_a(3, 1, CUT_V)
    for rt in range(NRT):
        values = k_at(1, rt)
        lo, hi = p_blocks(rt)
        for b in range(lo, hi):
            at = slice(b * PB, (b + 1) * PB)
            dw = lax.dot_general(values, q_at(1, b, b + 1), NT, preferred_element_type=F32)
            ds_buf[rt, :, at] = (dw * f_buf[rt, :, at]).astype(BF16)
        acc = jnp.dot(ds_buf[rt, :, lo * PB:hi * PB], q_at(0, lo, hi), preferred_element_type=F32)
        put_keys_grad(1, rt, acc * (scale / ATT_DIV))
    for n, (rows, _, _) in enumerate(CUT_DK):
        send_a2(1, *rows, rs_a2.at[1, n])
    for n, (rows, _, _) in enumerate(CUT_DV):
        send_b2(0, *rows, rs_a2.at[0, n], rb2.at[0], rs_b2.at[0, n])
    rb2[0, z] = sb2[0, z]

    dq_view = dq_buf.reshape(2, NM, 2, PADH, HD)

    def swap(half):
        return pltpu.make_async_remote_copy(
            src_ref=xs.at[half], dst_ref=xr.at[half], send_sem=sent.at[3], recv_sem=rs_x.at[half],
            device_id=twin, device_id_type=MESH)

    for half in range(2):
        for b in range(half * NPB // 2, (half + 1) * NPB // 2):
            acc = jnp.zeros((HD, PB), F32)
            for rt in range(NRT):
                lo, hi = p_blocks(rt)
                if lo <= b < hi:
                    acc = acc + jnp.dot(
                        kt[rt], ds_buf[rt, :, b * PB:(b + 1) * PB], preferred_element_type=F32)
            dq_buf[b * PB:(b + 1) * PB, :] = acc.T * (scale / ATT_DIV)
        xs[half] = dq_view[half, :, 1 - kap]
        swap(half).start()
    for half in range(2):
        swap(half).wait_recv()
        for mm in range(NM):
            g2[2, half * NM + mm] = (dq_view[half, mm, kap] + xr[half, mm]).astype(BF16)
    for n, (rows, _, _) in enumerate(CUT_DQ):
        send_a2(2, *rows, rs_a2.at[2, n])
    for n, (rows, _, _) in enumerate(CUT_DK):
        send_b2(1, *rows, rs_a2.at[1, n], rb2.at[1], rs_b2.at[1, n])
    rb2[1, z] = sb2[1, z]
    for n, (rows, _, _) in enumerate(CUT_DQ):
        send_b2(2, *rows, rs_a2.at[2, n], oq_ref, rs_b2.at[2, n])
    keep = pltpu.make_async_copy(sb2.at[2, z], oq_ref.at[z], out_sem.at[2])
    keep.start()
    stores.append(keep)

    def home(g, cut, dst):
        for n, (_, (lo, hi), _) in enumerate(cut):
            wait_b(sb2.at[g], dst, lo, hi, sent.at[5], rs_b2.at[g, n])

    for g, out in enumerate((ov_ref, ok_ref)):
        home(g, (CUT_DV, CUT_DK)[g], rb2.at[g])
        done[g] = unpack(rb2.at[g], scr, to_arrival)
        stores.append(pltpu.make_async_copy(done.at[g], out, out_sem.at[g]))
        stores[-1].start()
    home(2, CUT_DQ, oq_ref)

    for n, part in enumerate((
        sb.at[pl.ds(0, NZ - 1)], sa.at[:, pl.ds(0, NXY - 1)], events.at[pl.ds(0, 2), :, :, 0], xs,
        g2.at[:, pl.ds(0, NXY - 1)], sb2.at[:, pl.ds(0, NZ - 1)],
    )):
        pltpu.make_async_remote_copy(
            src_ref=part, dst_ref=part, send_sem=sent.at[n], recv_sem=rs_x.at[0],
            device_id=twin, device_id_type=MESH).wait_send()
    for store in stores:
        store.wait()


def finish(tgt, q_ref, k_ref, v_ref, u_ref, oq_ref, ok_ref, ov_ref, ou_ref, blocks, rows, scr, sems):
    ins = [pltpu.make_async_copy(q_ref, blocks, sems.at[0])]
    outs = []
    for n, (ref, out) in enumerate(((k_ref, ok_ref), (v_ref, ov_ref), (u_ref, ou_ref))):
        ins.append(pltpu.make_async_copy(ref, rows.at[n], sems.at[n + 1]))
        outs.append(pltpu.make_async_copy(rows.at[n], out, sems.at[n + 4]))
    for copy in ins:
        copy.start()
    _, to_arrival = one_hots(tgt)
    ins[0].wait()
    rows[3] = unpack(blocks, scr, to_arrival)
    outs.append(pltpu.make_async_copy(rows.at[3], oq_ref, sems.at[7]))
    outs[3].start()
    for n in range(3):
        ins[n + 1].wait()
        outs[n].start()
    for copy in outs:
        copy.wait()


def local(queries, keys, values, gates, attn_out, grad_out, route, lengths):
    hbm = pl.BlockSpec(memory_space=pl.ANY)
    smem = pl.BlockSpec(memory_space=pltpu.SMEM)
    dma = pltpu.SemaphoreType.DMA
    shape = jax.ShapeDtypeStruct((ROWS, D), BF16)
    attention = (NRT, RT, NPB * PB)
    outs = pl.pallas_call(
        kernel,
        name="hstu_backward",
        out_shape=[jax.ShapeDtypeStruct((NZ, NB, HD), BF16)] + [shape] * 3,
        in_specs=[smem] * 2 + [hbm] * 6,
        out_specs=[hbm] * 4,
        scratch_shapes=[
            pltpu.VMEM((6, ROWS, D), BF16),
            pltpu.VMEM((4, ROWS, D), BF16),
            pltpu.VMEM((ROWS * 16, HD), F32),
            pltpu.VMEM((NZ, 4 * NB, HD), BF16),
            pltpu.VMEM((NZ, 4 * NB, HD), BF16),
            pltpu.VMEM((4, NXY, PADH, HD), BF16),
            pltpu.VMEM((4, 2, NM, 2, PADH, HD), BF16),
            pltpu.VMEM((NRT, HD, RT), BF16),
            pltpu.VMEM(attention, BF16),
            pltpu.VMEM(attention, F32),
            pltpu.VMEM(attention, BF16),
            pltpu.VMEM((NPB * PB, HD), F32),
            pltpu.VMEM((2, NM, PADH, HD), F32),
            pltpu.VMEM((2, NM, PADH, HD), F32),
            pltpu.VMEM((3, NXY, PADH, HD), BF16),
            pltpu.VMEM((3, NXY, PADH, HD), BF16),
            pltpu.VMEM((3, NZ, NB, HD), BF16),
            pltpu.VMEM((2, NZ, NB, HD), BF16),
            pltpu.VMEM((2, 8, NPB * PB), jnp.int32),
            dma((6,)), dma((4,)), dma((6,)),
            dma((6,)), dma((4, 2)), dma((3, 2)), dma((2,)), dma((3, 2)), dma((3, 2)),
        ],
        compiler_params=pltpu.CompilerParams(
            collective_id=0, has_side_effects=True, vmem_limit_bytes=56 * 1024 * 1024
        ),
        cost_estimate=pl.CostEstimate(flops=3_400_000_000, bytes_accessed=3_000_000, transcendentals=2_000_000),
    )(route, lengths, queries[0], keys[0], values[0], gates[0], attn_out[0], grad_out[0])
    outs = pl.pallas_call(
        finish,
        name="finish",
        out_shape=[shape] * 4,
        in_specs=[smem] + [hbm] * 4,
        out_specs=[hbm] * 4,
        scratch_shapes=[
            pltpu.VMEM((NZ, NB, HD), BF16),
            pltpu.VMEM((4, ROWS, D), BF16),
            pltpu.VMEM((ROWS * HEADS, HD), F32),
            dma((8,)),
        ],
        compiler_params=pltpu.CompilerParams(vmem_limit_bytes=56 * 1024 * 1024),
    )(route, *outs)
    return tuple(x[None] for x in outs)


def solution(mesh):
    rows = P("dp", "ctx", None)
    return jax.shard_map(
        local,
        mesh=mesh,
        in_specs=(rows,) * 6 + (P("dp", "ctx"), P("dp", None)),
        out_specs=(rows,) * 4,
        check_vma=False,
    )
```

```python
import math

import jax
import jax.numpy as jnp
from jax import lax
from jax.experimental import pallas as pl
from jax.experimental.pallas import tpu as pltpu
from jax.sharding import PartitionSpec as P

D = 1024
HEADS = 8
HD = 128
ROWS = 144
HALF = 72
PADH = 80
BLK = 9
NDP = 16
NZ = 8
NCTX = 16
NM = 8
USERS = 4
ATT_DIV = 32
RT = 160
PB = 256
NRT = 8
NPB = 10
NXY = 16
NB = 2 * BLK * HEADS
Z_STEPS = (4, 3, 5, 2, 6, 1, 7)
MESH = pl.DeviceIdType.MESH
F32 = jnp.float32
BF16 = jnp.bfloat16
NT = (((1,), (1,)), ((), ()))

GROUPS = ((0, 4, 0, 32), (4, 9, 32, 80))
WHOLE = (0, PADH)
PARTS = ((0, 32), (32, 80))
B_PARTS = ((0, 64), (64, NB))
IN_ONE = (((0, PADH), (0, NB), GROUPS),)
IN_TWO = (((0, 32), (0, 64), GROUPS[:1]), ((32, PADH), (64, NB), GROUPS[1:]))
CUT_QK, CUT_DO, CUT_V, CUT_DV, CUT_DK, CUT_DQ = IN_TWO, IN_ONE, IN_TWO, IN_TWO, IN_ONE, IN_ONE


def p_blocks(rt):
    return (rt, NPB) if rt < 4 else (5, 7 + rt - 4)


def inner_place(x):
    y = x - 32
    block = (y * 205) // 1024
    return jnp.where(x < 32, (x // 4) * BLK + x % 4, block * BLK + 4 + y - 5 * block)


def one_hots(tgt):
    row = lax.broadcasted_iota(jnp.int32, (ROWS, ROWS), 0)
    col = lax.broadcasted_iota(jnp.int32, (ROWS, ROWS), 1)
    shift_c = jnp.zeros((ROWS, ROWS), jnp.int32)
    shift_r = jnp.zeros((ROWS, ROWS), jnp.int32)
    for b in range(NDP):
        by = (tgt[0, b] - b) * BLK
        shift_c = jnp.where((col >= b * BLK) & (col < b * BLK + BLK), by, shift_c)
        shift_r = jnp.where((row >= b * BLK) & (row < b * BLK + BLK), by, shift_r)
    to_stream = jnp.where(row == col + shift_c, 1.0, 0.0).astype(BF16)
    to_arrival = jnp.where(col == row + shift_r, 1.0, 0.0).astype(BF16)
    return to_stream, to_arrival


def unpack(blocks, scr, to_arrival):
    for other in range(NZ):
        x = blocks[other].astype(F32)
        for stream in range(2):
            at = (stream * NZ + other) * HALF
            scr[at:at + 32, :] = x[stream * 32:stream * 32 + 32]
            scr[at + 32:at + HALF, :] = x[64 + stream * 40:104 + stream * 40]
    rows = jnp.concatenate(
        [scr[pl.ds(h, ROWS, stride=HEADS), :].astype(BF16) for h in range(HEADS)], axis=1)
    return jnp.dot(to_arrival, rows, preferred_element_type=F32).astype(BF16)


def kernel(
    tgt, lens, q_ref, k_ref, v_ref, u_ref, o_ref, dy_ref,
    oq_ref, ok_ref, ov_ref, ou_ref,
    held, done, scr, sb, rb, sa, events, kt, w_buf, f_buf, ds_buf,
    dq_buf, xs, xr, g2, r2, sb2, rb2, at_query,
    in_sem, out_sem, sent, rs_b, rs_a, rs_f, rs_x, rs_a2, rs_b2,
):
    dp = lax.axis_index("dp")
    ctx = lax.axis_index("ctx")
    xlo, z = dp // NZ, dp % NZ
    m, kap = ctx // 2, ctx % 2
    scale = 1.0 / math.sqrt(HD)
    twin = (dp, m * 2 + 1 - kap)

    def z_peer(d):
        return lax.rem(z + d, NZ)

    def at_z(other):
        return (xlo * NZ + other, ctx)

    def xy_peer(e):
        return lax.rem(xlo + e, 2) * NM + lax.rem(m + lax.div(e, 2), NM)

    def at_xy(unit):
        return (lax.div(unit, NM) * NZ + z, lax.rem(unit, NM) * 2 + kap)

    mine = xlo * NM + m

    def loop(lo, hi, body):
        def step(i, c):
            body(i)
            return c

        lax.fori_loop(lo, hi, step, 0, unroll=True)

    loads = [
        pltpu.make_async_copy(ref, held.at[n], in_sem.at[n])
        for n, ref in enumerate((q_ref, k_ref, o_ref, dy_ref, u_ref, v_ref))
    ]
    for load in loads:
        load.start()

    barrier = pltpu.get_barrier_semaphore()
    for d in Z_STEPS:
        pl.semaphore_signal(barrier, inc=1, device_id=at_z(z_peer(d)), device_id_type=MESH)
    loop(1, NXY, lambda e: pl.semaphore_signal(
        barrier, inc=1, device_id=at_xy(xy_peer(e)), device_id_type=MESH))
    pl.semaphore_signal(barrier, inc=1, device_id=twin, device_id_type=MESH)

    to_stream, to_arrival = one_hots(tgt)

    def pack_b(arrays, lo):
        n = len(arrays) * HEADS
        for a, x in enumerate(arrays):
            y = jnp.dot(to_stream, x, preferred_element_type=F32)
            for h in range(HEADS):
                scr[pl.ds(a * HEADS + h, ROWS, stride=n), :] = y[:, h * HD:(h + 1) * HD]
        for other in range(NZ):
            pieces = []
            for first, last, _, _ in GROUPS:
                for stream in range(2):
                    at = (stream * NZ + other) * BLK * n
                    pieces.append(scr[at + first * n:at + last * n, :])
            sb[other, lo:lo + 2 * BLK * n] = jnp.concatenate(pieces, axis=0).astype(BF16)

    def send_b(src, dst, lo, hi, send_sem, recv_sem):
        rows = pl.ds(lo, hi - lo)

        def step(d):
            other = z_peer(d)
            pltpu.make_async_remote_copy(
                src_ref=src.at[other, rows], dst_ref=dst.at[z, rows], send_sem=send_sem, recv_sem=recv_sem,
                device_id=at_z(other), device_id_type=MESH).start()

        for d in Z_STEPS:
            step(d)

    def wait_b(src, dst, lo, hi, send_sem, recv_sem):
        part = (pl.ds(0, NZ - 1), pl.ds(lo, hi - lo))
        pltpu.make_async_remote_copy(
            src_ref=src.at[part], dst_ref=dst.at[part], send_sem=send_sem, recv_sem=recv_sem,
            device_id=at_z(z_peer(1)), device_id_type=MESH).wait_recv()

    zeros8 = jnp.zeros((8, HD), F32)

    def pack_a(lo, arrays, group):
        n = len(arrays) * HEADS
        first, last, at, end = group
        r = last - first
        base = lo + 2 * first * n
        for other in range(NZ):
            x = rb[other, base:base + 2 * r * n].astype(F32)
            for stream in range(2):
                at_scr = (stream * NZ + other) * r * n
                scr[at_scr:at_scr + r * n, :] = x[stream * r * n:(stream + 1) * r * n]
        for a, arr in enumerate(arrays):
            for h in range(HEADS):
                x = scr[pl.ds(a * HEADS + h, NDP * r, stride=n), :]
                for stream in range(2):
                    y = x[stream * 8 * r:(stream + 1) * 8 * r]
                    if end - at > 8 * r:
                        y = jnp.concatenate([y, zeros8], axis=0)
                    sa[arr, stream * NM + h, at:end] = y.astype(BF16)

    def send_a(arr, n, lo, hi, recv_sem):
        arrs, rows = pl.ds(arr, n), pl.ds(lo, hi - lo)

        def step(e):
            unit = xy_peer(e)
            pltpu.make_async_remote_copy(
                src_ref=sa.at[arrs, unit, rows], dst_ref=events.at[arrs, xlo, m, kap, rows],
                send_sem=sent.at[1], recv_sem=recv_sem, device_id=at_xy(unit), device_id_type=MESH).start()

        loop(1, NXY, step)
        events[arrs, xlo, m, kap, rows] = sa[arrs, mine, rows]

    def wait_a(arr, n, lo, hi, recv_sem):
        part = sa.at[pl.ds(arr, n), pl.ds(0, NXY - 1), pl.ds(lo, hi - lo)]
        pltpu.make_async_remote_copy(
            src_ref=part, dst_ref=part, send_sem=sent.at[1], recv_sem=recv_sem,
            device_id=at_xy(xy_peer(jnp.int32(1))), device_id_type=MESH).wait_recv()

    def share(arr, par, lo, hi, recv_sem):
        ref = events.at[arr, :, :, par, pl.ds(lo, hi - lo)]
        return pltpu.make_async_remote_copy(
            src_ref=ref, dst_ref=ref, send_sem=sent.at[2], recv_sem=recv_sem,
            device_id=twin, device_id_type=MESH)

    def send_a2(g, lo, hi, recv_sem):
        rows = pl.ds(lo, hi - lo)

        def step(e):
            unit = xy_peer(e)
            pltpu.make_async_remote_copy(
                src_ref=g2.at[g, unit, rows], dst_ref=r2.at[g, mine, rows], send_sem=sent.at[4], recv_sem=recv_sem,
                device_id=at_xy(unit), device_id_type=MESH).start()

        loop(1, NXY, step)
        r2[g, mine, rows] = g2[g, mine, rows]

    def send_b2(g, lo, hi, from_sem, dst, recv_sem):
        part = r2.at[g, pl.ds(0, NXY - 1), pl.ds(lo, hi - lo)]
        pltpu.make_async_remote_copy(
            src_ref=part, dst_ref=part, send_sem=sent.at[4], recv_sem=from_sem,
            device_id=at_xy(xy_peer(jnp.int32(1))), device_id_type=MESH).wait_recv()
        for first, last, at, end in GROUPS:
            if lo <= at < hi:
                r = last - first
                n = r * HEADS
                for stream in range(2):
                    for h in range(HEADS):
                        scr[pl.ds(stream * NZ * n + h, 8 * r, stride=HEADS), :] = (
                            r2[g, stream * NM + h, at:end].astype(F32)[:8 * r])
                for other in range(NZ):
                    sb2[g, other, 2 * at:2 * at + 2 * n] = jnp.concatenate(
                        [scr[(stream * NZ + other) * n:(stream * NZ + other + 1) * n, :] for stream in range(2)],
                        axis=0).astype(BF16)
        low, high = 2 * lo, min(2 * hi, NB)
        send_b(sb2.at[g], dst, low, high, sent.at[5], recv_sem)

    loads[0].wait()
    loads[1].wait()
    pack_b([held[0], held[1]], 0)
    pl.semaphore_wait(barrier, NZ - 1 + NXY - 1 + 1)
    b_qk = [(sb, rb, 2 * lo, 2 * hi, sent.at[0], rs_b.at[n]) for n, (_, (lo, hi), _) in enumerate(CUT_QK)]
    for part in b_qk:
        send_b(*part)
    rb[z, :2 * NB] = sb[z, :2 * NB]

    for load in loads[2:5]:
        load.wait()
    o_full = held[2].astype(F32)
    centred = o_full - jnp.mean(o_full, axis=1, keepdims=True)
    inv_std = 1.0 / jnp.sqrt(jnp.mean(centred * centred, axis=1, keepdims=True) + 1e-05)
    normed = centred * inv_std
    dy_full = held[3].astype(F32)
    done[3] = (dy_full * normed).astype(BF16)
    stores = [pltpu.make_async_copy(done.at[3], ou_ref, out_sem.at[3])]
    stores[0].start()
    g_term = dy_full * held[4].astype(F32)
    d_o = inv_std * (
        g_term
        - jnp.mean(g_term, axis=1, keepdims=True)
        - normed * jnp.mean(g_term * normed, axis=1, keepdims=True)
    )
    at_do, at_v = 2 * NB, 3 * NB
    pack_b([d_o.astype(BF16)], at_do)
    b_do = [(sb, rb, at_do + lo, at_do + hi, sent.at[0], rs_b.at[2 + n]) for n, (_, (lo, hi), _) in enumerate(CUT_DO)]
    for part in b_do:
        send_b(*part)
    loads[5].wait()
    pack_b([held[5]], at_v)
    b_v = [(sb, rb, at_v + lo, at_v + hi, sent.at[0], rs_b.at[4 + n]) for n, (_, (lo, hi), _) in enumerate(CUT_V)]
    for part in b_v:
        send_b(*part)
    rb[z, at_do:] = sb[z, at_do:]

    ends = []
    total = jnp.int32(0)
    for user in range(USERS):
        total = total + lens[0, user]
        ends.append(total)
    lane = lax.broadcasted_iota(jnp.int32, (8, NPB * PB), 1)
    late = lane >= NCTX * PADH
    lane_in = lane - jnp.where(late, NCTX * PADH, 0)
    chunk = jnp.zeros_like(lane_in)
    for c in range(1, NCTX):
        chunk = chunk + jnp.where(lane_in >= c * PADH, 1, 0)
    place = jnp.where(late, 2 * NCTX - 1 - chunk, chunk) * HALF + inner_place(lane_in - chunk * PADH)
    first = jnp.zeros_like(place)
    for user in range(USERS - 1):
        first = jnp.maximum(first, jnp.where(ends[user] <= place, ends[user], 0))
    at_query[0] = place
    at_query[1] = first

    sub = lax.broadcasted_iota(jnp.int32, (RT, PB), 0)
    second = jnp.where(sub >= PADH, 1, 0)
    key_inner = inner_place(sub - second * PADH)

    def key_places(rt):
        c = 2 * (2 * (rt % 4) + second) + kap
        return (c if rt < 4 else 2 * NCTX - 1 - c) * HALF + key_inner

    def q_at(a, lo, hi):
        return events.at[2 * a].reshape(2 * NCTX * PADH, HD)[lo * PB:hi * PB, :]

    def k_at(a, rt):
        half, t = rt // 4, rt % 4
        return jnp.concatenate([events[2 * a + 1, half, 2 * t + n, kap] for n in range(2)], axis=0)

    def get_b(parts, cut, n, lo, arrays):
        rows, _, groups = cut[n]
        wait_b(*parts[n])
        for group in groups:
            pack_a(lo, arrays, group)
        send_a(arrays[0], len(arrays), *rows, rs_a.at[arrays[0], n])

    def get_a(arr, count, cut):
        for n, (rows, _, _) in enumerate(cut):
            wait_a(arr, count, *rows, rs_a.at[arr, n])
            if arr < 3:
                share(arr, kap, *rows, rs_f.at[arr, n]).start()

    def get_share(arr, cut):
        for n, (rows, _, _) in enumerate(cut):
            share(arr, 1 - kap, *rows, rs_f.at[arr, n]).wait_recv()

    for n in range(len(CUT_QK)):
        get_b(b_qk, CUT_QK, n, 0, [0, 1])
    for n in range(len(CUT_DO)):
        get_b(b_do, CUT_DO, n, at_do, [2])
    get_a(0, 2, CUT_QK)
    get_share(0, CUT_QK)

    for rt in range(NRT):
        keys = k_at(0, rt)
        kt[rt] = keys.T
        key_place = key_places(rt)
        for b in range(*p_blocks(rt)):
            at = slice(b * PB, (b + 1) * PB)
            s = lax.dot_general(keys, q_at(0, b, b + 1), NT, preferred_element_type=F32) * scale
            sig = 0.5 * jnp.tanh(0.5 * s) + 0.5
            live = (key_place <= at_query[0, :1, at]) & (key_place >= at_query[1, :1, at])
            sig = jnp.where(live, sig, 0.0)
            w = s * sig
            w_buf[rt, :, at] = w.astype(BF16)
            f_buf[rt, :, at] = sig * (1.0 - w) + w

    get_b(b_v, CUT_V, 0, at_v, [3])
    get_a(2, 1, CUT_DO)
    get_b(b_v, CUT_V, 1, at_v, [3])
    get_share(2, CUT_DO)

    def put_keys_grad(g, rt, value):
        t, half = rt % 4, rt // 4
        g2[g, half * NM + 2 * t] = value[:PADH].astype(BF16)
        g2[g, half * NM + 2 * t + 1] = value[PADH:].astype(BF16)

    for rt in range(NRT):
        lo, hi = p_blocks(rt)
        acc = jnp.dot(w_buf[rt, :, lo * PB:hi * PB], q_at(1, lo, hi), preferred_element_type=F32)
        put_keys_grad(0, rt, acc * (1.0 / ATT_DIV))
    for n, (rows, _, _) in enumerate(CUT_DV):
        send_a2(0, *rows, rs_a2.at[0, n])

    get_a(3, 1, CUT_V)
    for rt in range(NRT):
        values = k_at(1, rt)
        lo, hi = p_blocks(rt)
        for b in range(lo, hi):
            at = slice(b * PB, (b + 1) * PB)
            dw = lax.dot_general(values, q_at(1, b, b + 1), NT, preferred_element_type=F32)
            ds_buf[rt, :, at] = (dw * f_buf[rt, :, at]).astype(BF16)
        acc = jnp.dot(ds_buf[rt, :, lo * PB:hi * PB], q_at(0, lo, hi), preferred_element_type=F32)
        put_keys_grad(1, rt, acc * (scale / ATT_DIV))
    for n, (rows, _, _) in enumerate(CUT_DK):
        send_a2(1, *rows, rs_a2.at[1, n])
    for n, (rows, _, _) in enumerate(CUT_DV):
        send_b2(0, *rows, rs_a2.at[0, n], rb2.at[0], rs_b2.at[0, n])
    rb2[0, z] = sb2[0, z]

    dq_view = dq_buf.reshape(2, NM, 2, PADH, HD)

    def swap(half):
        return pltpu.make_async_remote_copy(
            src_ref=xs.at[half], dst_ref=xr.at[half], send_sem=sent.at[3], recv_sem=rs_x.at[half],
            device_id=twin, device_id_type=MESH)

    for half in range(2):
        for b in range(half * NPB // 2, (half + 1) * NPB // 2):
            acc = jnp.zeros((HD, PB), F32)
            for rt in range(NRT):
                lo, hi = p_blocks(rt)
                if lo <= b < hi:
                    acc = acc + jnp.dot(
                        kt[rt], ds_buf[rt, :, b * PB:(b + 1) * PB], preferred_element_type=F32)
            dq_buf[b * PB:(b + 1) * PB, :] = acc.T * (scale / ATT_DIV)
        xs[half] = dq_view[half, :, 1 - kap]
        swap(half).start()
    for half in range(2):
        swap(half).wait_recv()
        for mm in range(NM):
            g2[2, half * NM + mm] = (dq_view[half, mm, kap] + xr[half, mm]).astype(BF16)
    for n, (rows, _, _) in enumerate(CUT_DQ):
        send_a2(2, *rows, rs_a2.at[2, n])
    for n, (rows, _, _) in enumerate(CUT_DK):
        send_b2(1, *rows, rs_a2.at[1, n], rb2.at[1], rs_b2.at[1, n])
    rb2[1, z] = sb2[1, z]
    for n, (rows, _, _) in enumerate(CUT_DQ):
        send_b2(2, *rows, rs_a2.at[2, n], oq_ref, rs_b2.at[2, n])
    keep = pltpu.make_async_copy(sb2.at[2, z], oq_ref.at[z], out_sem.at[2])
    keep.start()
    stores.append(keep)

    def home(g, cut, dst):
        for n, (_, (lo, hi), _) in enumerate(cut):
            wait_b(sb2.at[g], dst, lo, hi, sent.at[5], rs_b2.at[g, n])

    for g, out in enumerate((ov_ref, ok_ref)):
        home(g, (CUT_DV, CUT_DK)[g], rb2.at[g])
        done[g] = unpack(rb2.at[g], scr, to_arrival)
        stores.append(pltpu.make_async_copy(done.at[g], out, out_sem.at[g]))
        stores[-1].start()
    home(2, CUT_DQ, oq_ref)

    for n, part in enumerate((
        sb.at[pl.ds(0, NZ - 1)], sa.at[:, pl.ds(0, NXY - 1)], events.at[pl.ds(0, 2), :, :, 0], xs,
        g2.at[:, pl.ds(0, NXY - 1)], sb2.at[:, pl.ds(0, NZ - 1)],
    )):
        pltpu.make_async_remote_copy(
            src_ref=part, dst_ref=part, send_sem=sent.at[n], recv_sem=rs_x.at[0],
            device_id=twin, device_id_type=MESH).wait_send()
    for store in stores:
        store.wait()


def finish(tgt, q_ref, k_ref, v_ref, u_ref, oq_ref, ok_ref, ov_ref, ou_ref, blocks, rows, scr, sems):
    ins = [pltpu.make_async_copy(q_ref, blocks, sems.at[0])]
    outs = []
    for n, (ref, out) in enumerate(((k_ref, ok_ref), (v_ref, ov_ref), (u_ref, ou_ref))):
        ins.append(pltpu.make_async_copy(ref, rows.at[n], sems.at[n + 1]))
        outs.append(pltpu.make_async_copy(rows.at[n], out, sems.at[n + 4]))
    for copy in ins:
        copy.start()
    _, to_arrival = one_hots(tgt)
    ins[0].wait()
    rows[3] = unpack(blocks, scr, to_arrival)
    outs.append(pltpu.make_async_copy(rows.at[3], oq_ref, sems.at[7]))
    outs[3].start()
    for n in range(3):
        ins[n + 1].wait()
        outs[n].start()
    for copy in outs:
        copy.wait()


def local(queries, keys, values, gates, attn_out, grad_out, route, lengths):
    hbm = pl.BlockSpec(memory_space=pl.ANY)
    smem = pl.BlockSpec(memory_space=pltpu.SMEM)
    dma = pltpu.SemaphoreType.DMA
    shape = jax.ShapeDtypeStruct((ROWS, D), BF16)
    attention = (NRT, RT, NPB * PB)
    outs = pl.pallas_call(
        kernel,
        name="hstu_backward",
        out_shape=[jax.ShapeDtypeStruct((NZ, NB, HD), BF16)] + [shape] * 3,
        in_specs=[smem] * 2 + [hbm] * 6,
        out_specs=[hbm] * 4,
        scratch_shapes=[
            pltpu.VMEM((6, ROWS, D), BF16),
            pltpu.VMEM((4, ROWS, D), BF16),
            pltpu.VMEM((ROWS * 16, HD), F32),
            pltpu.VMEM((NZ, 4 * NB, HD), BF16),
            pltpu.VMEM((NZ, 4 * NB, HD), BF16),
            pltpu.VMEM((4, NXY, PADH, HD), BF16),
            pltpu.VMEM((4, 2, NM, 2, PADH, HD), BF16),
            pltpu.VMEM((NRT, HD, RT), BF16),
            pltpu.VMEM(attention, BF16),
            pltpu.VMEM(attention, F32),
            pltpu.VMEM(attention, BF16),
            pltpu.VMEM((NPB * PB, HD), F32),
            pltpu.VMEM((2, NM, PADH, HD), F32),
            pltpu.VMEM((2, NM, PADH, HD), F32),
            pltpu.VMEM((3, NXY, PADH, HD), BF16),
            pltpu.VMEM((3, NXY, PADH, HD), BF16),
            pltpu.VMEM((3, NZ, NB, HD), BF16),
            pltpu.VMEM((2, NZ, NB, HD), BF16),
            pltpu.VMEM((2, 8, NPB * PB), jnp.int32),
            dma((6,)), dma((4,)), dma((6,)),
            dma((6,)), dma((4, 2)), dma((3, 2)), dma((2,)), dma((3, 2)), dma((3, 2)),
        ],
        compiler_params=pltpu.CompilerParams(
            collective_id=0, has_side_effects=True, vmem_limit_bytes=56 * 1024 * 1024
        ),
        cost_estimate=pl.CostEstimate(flops=3_400_000_000, bytes_accessed=3_000_000, transcendentals=2_000_000),
    )(route, lengths, queries[0], keys[0], values[0], gates[0], attn_out[0], grad_out[0])
    outs = pl.pallas_call(
        finish,
        name="finish",
        out_shape=[shape] * 4,
        in_specs=[smem] + [hbm] * 4,
        out_specs=[hbm] * 4,
        scratch_shapes=[
            pltpu.VMEM((NZ, NB, HD), BF16),
            pltpu.VMEM((4, ROWS, D), BF16),
            pltpu.VMEM((ROWS * HEADS, HD), F32),
            dma((8,)),
        ],
        compiler_params=pltpu.CompilerParams(vmem_limit_bytes=56 * 1024 * 1024),
    )(route, *outs)
    return tuple(x[None] for x in outs)


def solution(mesh):
    rows = P("dp", "ctx", None)
    return jax.shard_map(
        local,
        mesh=mesh,
        in_specs=(rows,) * 6 + (P("dp", "ctx"), P("dp", None)),
        out_specs=(rows,) * 4,
        check_vma=False,
    )
```
